128 devices in a mesh: dp: 16 (over x, z_hi, core), tm: 8 (over y, z_lo).
Axes of the slice: x: 4, y: 4, z: 4 (z_hi: 2, z_lo: 2; z = z_hi * 2 + z_lo), core: 2. Of those that a mesh axis runs over, the one named last changes fastest.
Arguments:
- video_tokens: bfloat16 [16, 2048, 1408], P('dp', 'tm'), may hold values from -6 to 6
- text_tokens: bfloat16 [2048, 64, 1024], P(('dp', 'tm')), may hold values from -6 to 6
- block_lists: int32 [16, 8, 8], P('dp', 'tm'), may hold values from -1 to 7, as said below
- positive_text: int32 [16], P('dp'), may hold values from 0 to 2047
- video_gain: float32 [1408], replicated, may hold values from 0.5 to 1.5
- w_video_qkv: bfloat16 [1408, 4224], P(('dp', 'tm')), may hold values from -0.15625 to 0.15625
- w_video_out: bfloat16 [1408, 1408], P(('dp', 'tm')), may hold values from -0.15625 to 0.15625
- text_gain: float32 [1024], replicated, may hold values from 0.5 to 1.5
- w_text_qkv: bfloat16 [1024, 3072], P(('dp', 'tm')), may hold values from -0.1875 to 0.1875
- w_text_out: bfloat16 [1024, 1024], P(('dp', 'tm')), may hold values from -0.1875 to 0.1875
- w_embed: bfloat16 [1408, 1024], P(('dp', 'tm')), may hold values from -0.15625 to 0.15625
- gem_power: float32 [1], replicated, may hold values from 2 to 4
- log_scale: float32 [1], replicated, may hold values from 2.2 to 2.8
- logit_bias: float32 [1], replicated, may hold values from -2 to 0
Outputs:
- video_out: bfloat16 [16, 2048, 1408], P('dp', 'tm')
- video_embed: float32 [16, 1024], P('dp')
- text_embed: float32 [2048, 1024], P(('dp', 'tm'))
- clip_loss: float32 [16], P('dp')
The draws below stay inside these ranges and needn't reach their ends.
Inputs may be any that keep to these rules, and one draw needn't show every extreme that they name: `block_lists`: row [c, q] lists first q itself, then distinct other time blocks, then -1 in the unused slots; the number of listed blocks varies from row to row, and some row lists all 8 blocks.
All inputs are finite; a program needn't handle non-finite values.
Results may differ from the reference program's by a relative error of at most 0.0054.
Values may be sent and summed in bfloat16 or wider, within the bound.
No kernel may reach another device: no remote copies, remote signals or barrier semaphores. Data moves between devices by JAX's collectives and lax.ppermute only.
A program may use at most 192 MiB of HBM per device.

```python
import jax
import jax.numpy as jnp
from jax import lax

D = 1408
VHEADS = 16
TD = 1024
THEADS = 16
TXT_DEV = 16
TLEN = 64
TOKV = 256
NBLK = 8
VTOK = 2048
CLIPS = 16
TEXTS = 2048


def draw_block_lists(key, part):
    key = jax.random.fold_in(key, 11)
    key_order, key_count = jax.random.split(key)
    orders = jax.vmap(lambda k: jax.random.permutation(k, NBLK))(jax.random.split(key_order, CLIPS * NBLK))
    ranks = orders.reshape(CLIPS, NBLK, NBLK).astype(jnp.int32)
    slots = jnp.arange(NBLK, dtype=jnp.int32)
    itself = slots[None, :, None] == slots[None, None, :]
    ranks = jnp.where(itself, -1, ranks)
    listed = jnp.argsort(ranks, axis=-1, stable=True).astype(jnp.int32)
    counts = jax.random.randint(key_count, (CLIPS, NBLK, 1), 1, NBLK + 1)
    first = (jnp.arange(CLIPS)[:, None, None] == 0) & (slots[None, :, None] == 0)
    counts = jnp.where(first, NBLK, counts)
    return jnp.where(slots[None, None, :] < counts, listed, -1).astype(jnp.int32)


def set_ends(entries, own_key, least, largest):
    place = [jax.random.randint(jax.random.fold_in(own_key, axis), (), 0, length) for axis, length in enumerate(entries.shape)]
    widest = entries.shape.index(max(entries.shape))
    beside = place[:widest] + [(place[widest] + 1) % entries.shape[widest]] + place[widest + 1:]
    return entries.at[tuple(place)].set(least).at[tuple(beside)].set(largest)


def steps_of(stream_key, extent, pieces, low, top_value):
    level = 1.0
    for axis_at, blocks in pieces:
        draws = jax.random.uniform(jax.random.fold_in(jax.random.fold_in(stream_key, 6), axis_at), (blocks,), jnp.float32, low / len(pieces), top_value / len(pieces))
        level = level * jnp.repeat(jnp.exp(draws), extent[axis_at] // blocks).reshape((-1,) + (1,) * (len(extent) - 1 - axis_at))
    return level


def normal_values(rng, extent, deviation, limit, cuts=(), kind=jnp.bfloat16):
    result = deviation * jax.random.normal(rng, extent, jnp.float32)
    if cuts:
        result = result * steps_of(rng, extent, cuts, -0.22, 0.18)
    return jnp.clip(result, -limit, limit).astype(kind)


def setup_inputs(seed: int = 0) -> dict:
    streams_of = jax.random.split(jax.random.key(seed), 15)
    video_tokens = normal_values(streams_of[0], (CLIPS, VTOK, D), 1.0, 6.0, ((0, 16), (1, 8)))
    text_tokens = normal_values(streams_of[1], (TEXTS, TLEN, TD), 1.0, 6.0, ((0, 128),))
    block_lists = draw_block_lists(jax.random.fold_in(streams_of[14], 71), 0)
    positive_text = set_ends(jax.random.randint(streams_of[3], (CLIPS,), 0, TEXTS), jax.random.fold_in(streams_of[3], 1), 0, TEXTS - 1).astype(jnp.int32)
    video_gain = jnp.clip(1.0 + 0.1 * jax.random.normal(streams_of[4], (D,), jnp.float32), 0.5, 1.5)
    w_video_qkv = normal_values(streams_of[5], (D, 3 * D), D ** -0.5, 0.15625, ((0, 128),))
    w_video_out = normal_values(streams_of[6], (D, D), D ** -0.5, 0.15625, ((0, 128),))
    text_gain = jnp.clip(1.0 + 0.1 * jax.random.normal(streams_of[7], (TD,), jnp.float32), 0.5, 1.5)
    w_text_qkv = normal_values(streams_of[8], (TD, 3 * TD), TD ** -0.5, 0.1875, ((0, 128),))
    w_text_out = normal_values(streams_of[9], (TD, TD), TD ** -0.5, 0.1875, ((0, 128),))
    w_embed = normal_values(streams_of[10], (D, TD), D ** -0.5, 0.15625, ((0, 128),))
    gem_power = jnp.clip(jax.random.uniform(streams_of[11], (1,), jnp.float32, 2.0, 4.0), 2.0, 4.0)
    log_scale = jnp.clip(jax.random.uniform(streams_of[12], (1,), jnp.float32, 2.2, 2.8), 2.2, 2.8)
    logit_bias = jnp.clip(jax.random.uniform(streams_of[13], (1,), jnp.float32, -2.0, 0.0), -2.0, 0.0)
    return {"video_tokens": video_tokens, "text_tokens": text_tokens, "block_lists": block_lists, "positive_text": positive_text, "video_gain": video_gain, "w_video_qkv": w_video_qkv, "w_video_out": w_video_out, "text_gain": text_gain, "w_text_qkv": w_text_qkv, "w_text_out": w_text_out, "w_embed": w_embed, "gem_power": gem_power, "log_scale": log_scale, "logit_bias": logit_bias}


def norm_rows(values, gain):
    full = values.astype(jnp.float32)
    scale = lax.rsqrt(lax.optimization_barrier(jnp.mean(full * full, axis=-1, keepdims=True)) + 1e-06)
    return (full * scale * gain).astype(jnp.bfloat16)

def attend(queries, keys, values, allowed, heads):
    count, width = queries.shape
    size = width // heads
    qh = queries.reshape(count, heads, size).astype(jnp.float32)
    kh = keys.reshape(keys.shape[0], heads, size).astype(jnp.float32)
    vh = values.reshape(values.shape[0], heads, size).astype(jnp.float32)
    scores = jnp.einsum('qhd,khd->hqk', qh, kh) / jnp.sqrt(jnp.float32(size))
    masked = jnp.where(allowed[None], scores, jnp.float32(-1e+30))
    top = lax.optimization_barrier(jnp.max(masked, axis=-1, keepdims=True))
    weights = jnp.exp(masked - top) * allowed[None].astype(jnp.float32)
    total = lax.optimization_barrier(jnp.sum(weights, axis=-1, keepdims=True))
    rounded = weights.astype(jnp.bfloat16).astype(jnp.float32)
    mixed = jnp.einsum('hqk,khd->hqd', rounded, vh) / total
    return jnp.transpose(mixed, (1, 0, 2)).reshape(count, width).astype(jnp.bfloat16)

def reference(video_tokens, text_tokens, block_lists, positive_text, video_gain, w_video_qkv, w_video_out, text_gain, w_text_qkv, w_text_out, w_embed, gem_power, log_scale, logit_bias):
    power = gem_power[0]

    def one_clip(inputs):
        tokens, lists = inputs
        normed = norm_rows(tokens, video_gain)
        qkv = jnp.dot(normed, w_video_qkv, preferred_element_type=jnp.float32).astype(jnp.bfloat16)
        queries, keys, values = (qkv[:, :D], qkv[:, D:2 * D], qkv[:, 2 * D:])
        blocks = jnp.arange(VTOK, dtype=jnp.int32) // TOKV
        seen = jnp.any(lists[:, :, None] == jnp.arange(NBLK, dtype=jnp.int32)[None, None, :], axis=1)
        allowed = seen[blocks][:, blocks]
        mixed = attend(queries, keys, values, allowed, VHEADS)
        out = (tokens.astype(jnp.float32) + jnp.dot(mixed, w_video_out, preferred_element_type=jnp.float32)).astype(jnp.bfloat16)
        sums = lax.optimization_barrier(jnp.sum(jnp.maximum(out.astype(jnp.float32), 1e-06) ** power, axis=0))
        pooled = ((sums / VTOK) ** (1.0 / power)).astype(jnp.bfloat16)
        proj = jnp.dot(pooled[None, :], w_embed, preferred_element_type=jnp.float32)[0]
        embed = proj * lax.rsqrt(jnp.sum(proj * proj) + 1e-06)
        return (out, embed)
    video_out, video_embed = lax.map(one_clip, (video_tokens, block_lists))
    groups = text_tokens.reshape(TEXTS // TXT_DEV, TXT_DEV, TLEN, TD)
    every = jnp.ones((TLEN, TLEN), dtype=bool)

    def text_group(tokens):
        flat = tokens.reshape(TXT_DEV * TLEN, TD)
        normed = norm_rows(flat, text_gain)
        qkv = jnp.dot(normed, w_text_qkv, preferred_element_type=jnp.float32).astype(jnp.bfloat16)
        qkv = qkv.reshape(TXT_DEV, TLEN, 3 * TD)
        mixed = jax.vmap(lambda rows: attend(rows[:, :TD], rows[:, TD:2 * TD], rows[:, 2 * TD:], every, THEADS))(qkv)
        out = (flat.astype(jnp.float32) + jnp.dot(mixed.reshape(TXT_DEV * TLEN, TD), w_text_out, preferred_element_type=jnp.float32)).astype(jnp.bfloat16)
        means = lax.optimization_barrier(jnp.mean(out.astype(jnp.float32).reshape(TXT_DEV, TLEN, TD), axis=1))
        return means * lax.rsqrt(lax.optimization_barrier(jnp.sum(means * means, axis=-1, keepdims=True)) + 1e-06)
    text_embed = lax.map(text_group, groups).reshape(TEXTS, TD)
    logits = jnp.exp(log_scale[0]) * jnp.dot(video_embed, text_embed.T, precision=lax.Precision.HIGHEST) + logit_bias[0]
    sign = jnp.where(jnp.arange(TEXTS, dtype=jnp.int32)[None, :] == positive_text[:, None], 1.0, -1.0)
    clip_loss = lax.optimization_barrier(jnp.sum(jax.nn.softplus(-sign * logits), axis=1)) / (TXT_DEV * NBLK)
    return (video_out, video_embed, text_embed, clip_loss)
```

```python
import functools

import jax
import jax.numpy as jnp
from jax import lax
from jax.experimental import pallas as pl
from jax.experimental.pallas import tpu as pltpu
from jax.sharding import Mesh
from jax.sharding import PartitionSpec as P

VHEADS = 16
THEADS = 16
HEAD = 88
LANES = 128
LOG2E = 1.4426950408889634

AXES = ("x", "h", "c", "y", "l")
DP = ("x", "h", "c")
TM = ("y", "l")
PLANE = ("c", "y", "l")


def norm_rows(values, gain):
    full = values.astype(jnp.float32)
    scale = lax.rsqrt(jnp.mean(full * full, axis=-1, keepdims=True) + 1e-06)
    return (full * scale * gain).astype(jnp.bfloat16)


def swap(value, axis):
    return lax.ppermute(value, axis, [(0, 1), (1, 0)])


def ordered_pair(own, other, index):
    first = jnp.where(index == 0, own, other)
    second = jnp.where(index == 0, other, own)
    return jnp.concatenate([first, second], axis=0)


def dot(a, b):
    return jnp.dot(a, b, preferred_element_type=jnp.float32)


def dot_t(a, b):
    return lax.dot_general(a, b, (((1,), (1,)), ((), ())), preferred_element_type=jnp.float32)


def video_attend_kernel(lists, slots, *refs):
    blocks = refs[:8]
    out_ref, qkv = refs[8], refs[9]
    for j in range(8):
        qkv[slots[j]] = blocks[j][...]
    factor = jnp.float32(LOG2E / HEAD**0.5)
    rows = out_ref.shape[1]

    def query_block(i, carry):
        count = jnp.int32(0)
        for k in range(8):
            count = count + jnp.where(lists[i, k] >= 0, 1, 0)

        def key_block(k, state):
            j = lists[i, k]
            new = []
            for head in range(2):
                top, total, acc = state[head]
                at = 3 * LANES * head
                q = qkv[i, :, at : at + LANES]
                key = qkv[j, :, at + LANES : at + 2 * LANES]
                value = qkv[j, :, at + 2 * LANES : at + 3 * LANES]
                s = dot_t(q, key)
                top_new = jnp.maximum(top, jnp.max(s, axis=1, keepdims=True))
                shift = top_new * factor
                w = jnp.exp2(s * factor - shift)
                old = jnp.exp2(top * factor - shift)
                part = w[:, :LANES] + w[:, LANES:]
                new.append((top_new, total * old + part, acc * old + dot(w.astype(jnp.bfloat16), value)))
            return tuple(new)

        zero = (
            jnp.full((rows, 1), -1e30, jnp.float32),
            jnp.zeros((rows, LANES), jnp.float32),
            jnp.zeros((rows, LANES), jnp.float32),
        )
        state = lax.fori_loop(0, count, key_block, (zero, zero))
        pad = jnp.zeros((rows, LANES), jnp.float32)
        mixed = []
        for head in range(2):
            _, total, acc = state[head]
            o = acc / jnp.sum(total, axis=1, keepdims=True)
            mixed.append(jnp.concatenate([o, pad], axis=1))
        both = mixed[0] + pltpu.roll(mixed[1], HEAD, 1)
        out_ref[i] = both[:, : 2 * HEAD].astype(jnp.bfloat16)
        return carry

    lax.fori_loop(0, 8, query_block, 0)


def video_attend(lists, slots, blocks):
    rows = blocks[0].shape[0]
    return pl.pallas_call(
        video_attend_kernel,
        out_shape=jax.ShapeDtypeStruct((8, rows, 2 * HEAD), jnp.bfloat16),
        in_specs=[pl.BlockSpec(memory_space=pltpu.SMEM)] * 2 + [pl.BlockSpec(memory_space=pltpu.VMEM)] * 8,
        out_specs=pl.BlockSpec(memory_space=pltpu.VMEM),
        scratch_shapes=[pltpu.VMEM((8, rows, 6 * LANES), jnp.bfloat16)],
        compiler_params=pltpu.CompilerParams(vmem_limit_bytes=40 * 2**20),
        cost_estimate=pl.CostEstimate(flops=5 * 10**9, bytes_accessed=4 * 10**6, transcendentals=5 * 10**6),
        name="video_attend",
    )(lists, slots, *blocks)


def video_out_kernel(core, power, mixed, tokens, own, other, out_ref, sums_ref, w, sems):
    c = core[0]
    first = pltpu.make_async_copy(own, w.at[c], sems.at[0])
    second = pltpu.make_async_copy(other, w.at[1 - c], sems.at[1])
    first.start()
    second.start()
    first.wait()
    second.wait()
    p = power[0]
    for half, (low, high, skip) in enumerate(((0, 768, 0), (768, 1408, 128))):
        acc = tokens[:, low:high].astype(jnp.float32)
        total = jnp.zeros_like(acc)
        for t in range(8):
            total = total + dot(mixed[t], w[half, 176 * t : 176 * (t + 1), 512 + skip :])
        out = (acc + total).astype(jnp.bfloat16)
        out_ref[:, low:high] = out
        grown = jnp.exp2(jnp.log2(jnp.maximum(out.astype(jnp.float32), 1e-06)) * p)
        sums_ref[:, low:high] = jnp.broadcast_to(jnp.sum(grown, axis=0, keepdims=True), (8, high - low))


def video_project(core, power, mixed, tokens, own, other):
    rows, width = tokens.shape
    vmem = pl.BlockSpec(memory_space=pltpu.VMEM)
    smem = pl.BlockSpec(memory_space=pltpu.SMEM)
    hbm = pl.BlockSpec(memory_space=pl.ANY)
    return pl.pallas_call(
        video_out_kernel,
        out_shape=(
            jax.ShapeDtypeStruct((rows, width), jnp.bfloat16),
            jax.ShapeDtypeStruct((8, width), jnp.float32),
        ),
        in_specs=[smem, smem, vmem, vmem, hbm, hbm],
        out_specs=(vmem, vmem),
        scratch_shapes=[pltpu.VMEM((2,) + own.shape, jnp.bfloat16), pltpu.SemaphoreType.DMA((2,))],
        compiler_params=pltpu.CompilerParams(vmem_limit_bytes=40 * 2**20),
        cost_estimate=pl.CostEstimate(flops=10**9, bytes_accessed=10**7, transcendentals=10**6),
        name="video_out",
    )(core, power, mixed, tokens, own, other)


def text_kernel(core, tokens_ref, gain_ref, own, other, embed_ref, w, mixed, sems):
    c = core[0]

    @pl.when(pl.program_id(0) == 0)
    def _():
        first = pltpu.make_async_copy(own, w.at[c], sems.at[0])
        second = pltpu.make_async_copy(other, w.at[1 - c], sems.at[1])
        first.start()
        second.start()
        first.wait()
        second.wait()

    rows, width = tokens_ref.shape
    half = width // 2
    length = 64
    tokens = tokens_ref[...].astype(jnp.float32)
    scale = lax.rsqrt(jnp.mean(tokens * tokens, axis=-1, keepdims=True) + 1e-06)
    normed = (tokens * scale * gain_ref[...]).astype(jnp.bfloat16)
    same = (lax.broadcasted_iota(jnp.int32, (rows, rows), 0) // length) == (
        lax.broadcasted_iota(jnp.int32, (rows, rows), 1) // length
    )
    low = lax.broadcasted_iota(jnp.int32, (rows, LANES), 1) < length
    factor = jnp.float32(LOG2E / 8.0)
    for side in range(2):
        qkv = dot(normed, w[side, :, : 3 * half]).astype(jnp.bfloat16)
        for pair in range(half // LANES):
            at = pair * LANES
            q = qkv[:, at : at + LANES]
            key = qkv[:, half + at : half + at + LANES]
            value = qkv[:, 2 * half + at : 2 * half + at + LANES]
            outs = []
            for head in range(2):
                mine = low if head == 0 else jnp.logical_not(low)
                s = dot_t(jnp.where(mine, q, jnp.zeros_like(q)), key)
                s = jnp.where(same, s, jnp.float32(-1e30))
                top = jnp.max(s, axis=1, keepdims=True)
                weights = jnp.exp2((s - top) * factor)
                total = jnp.sum(weights, axis=1, keepdims=True)
                outs.append(dot(weights.astype(jnp.bfloat16), value) / total)
            o = jnp.where(low, outs[0], outs[1])
            mixed[:, side * half + at : side * half + at + LANES] = o.astype(jnp.bfloat16)
    whole = mixed[...]
    means = []
    square = jnp.zeros((rows // length, 1), jnp.float32)
    for side in range(2):
        cols = slice(side * half, (side + 1) * half)
        projected = dot(whole, w[side, :, 3 * half :])
        out = (tokens_ref[:, cols].astype(jnp.float32) + projected).astype(jnp.bfloat16).astype(jnp.float32)
        mean = jnp.sum(out.reshape(rows // length, length, half), axis=1) * (1.0 / length)
        square = square + jnp.sum(mean * mean, axis=1, keepdims=True)
        means.append(mean)
    inverse = lax.rsqrt(square + 1e-06)
    for side in range(2):
        embed_ref[0, :, side * half : (side + 1) * half] = means[side] * inverse


def text_layer(core, tokens, gain, own, other):
    rows, width = tokens.shape
    step = 256
    smem = pl.BlockSpec(memory_space=pltpu.SMEM)
    hbm = pl.BlockSpec(memory_space=pl.ANY)
    out = pl.pallas_call(
        text_kernel,
        grid=(rows // step,),
        out_shape=jax.ShapeDtypeStruct((rows // step, step // 64, width), jnp.float32),
        in_specs=[
            smem,
            pl.BlockSpec((step, width), lambda i: (i, 0)),
            pl.BlockSpec((1, width), lambda i: (0, 0)),
            hbm,
            hbm,
        ],
        out_specs=pl.BlockSpec((1, step // 64, width), lambda i: (i, 0, 0)),
        scratch_shapes=[
            pltpu.VMEM((2,) + own.shape, jnp.bfloat16),
            pltpu.VMEM((step, width), jnp.bfloat16),
            pltpu.SemaphoreType.DMA((2,)),
        ],
        compiler_params=pltpu.CompilerParams(
            vmem_limit_bytes=48 * 2**20, dimension_semantics=("arbitrary",)
        ),
        cost_estimate=pl.CostEstimate(flops=17 * 10**9, bytes_accessed=10**7, transcendentals=4 * 10**6),
        name="text_layer",
    )(core, tokens, gain, own, other)
    return out.reshape(rows // 64, width)


def loss_kernel(ints, floats, sums, own, other, texts, embed_ref, loss_ref, *, tokens):
    c, t, positive = ints[0], ints[1], ints[2]
    total = jnp.sum(sums[...], axis=0, keepdims=True)
    pooled = jnp.exp(jnp.log(total * (1.0 / tokens)) * floats[0]).astype(jnp.bfloat16)
    pooled = jnp.broadcast_to(pooled, (16, pooled.shape[1]))
    mine = dot(pooled, own[...])[0:1]
    theirs = dot(pooled, other[...])[0:1]
    low = jnp.where(c == 0, mine, theirs)
    high = jnp.where(c == 0, theirs, mine)
    proj = jnp.concatenate([low, high], axis=1)
    embed = proj * lax.rsqrt(jnp.sum(proj * proj, axis=1, keepdims=True) + 1e-06)
    embed_ref[...] = embed
    count = texts.shape[0]
    logits = jnp.sum(texts[...] * embed, axis=1, keepdims=True) * floats[1] + floats[2]
    row = lax.broadcasted_iota(jnp.int32, (count, 1), 0)
    ids = (row // 16 * 8 + t) * 16 + row % 16
    z = jnp.where(ids == positive, -logits, logits)
    terms = jnp.maximum(z, 0.0) + jnp.log1p(jnp.exp(-jnp.abs(z)))
    loss_ref[...] = jnp.broadcast_to(jnp.sum(terms, axis=0, keepdims=True), loss_ref.shape)


def pooled_loss(ints, floats, sums, own, other, texts, tokens):
    smem = pl.BlockSpec(memory_space=pltpu.SMEM)
    whole = lambda a: pl.BlockSpec(a.shape, lambda i: (0, 0))
    width = texts.shape[1]
    embeds = pl.BlockSpec((own.shape[0], width // 2), lambda i: (0, 0))
    return pl.pallas_call(
        functools.partial(loss_kernel, tokens=tokens),
        grid=(1,),
        out_shape=(
            jax.ShapeDtypeStruct((1, width), jnp.float32),
            jax.ShapeDtypeStruct((8, LANES), jnp.float32),
        ),
        in_specs=[smem, smem, whole(sums), embeds, embeds, whole(texts)],
        out_specs=(
            pl.BlockSpec((1, width), lambda i: (0, 0)),
            pl.BlockSpec((8, LANES), lambda i: (0, 0)),
        ),
        compiler_params=pltpu.CompilerParams(vmem_limit_bytes=32 * 2**20),
        cost_estimate=pl.CostEstimate(flops=10**7, bytes_accessed=4 * 10**6, transcendentals=10**4),
        name="pooled_loss",
    )(ints, floats, sums, own, other, texts)


def pack_video(w_qkv, w_out, w_embed, listed):
    rows = w_qkv.shape[0]
    heads = jnp.pad(w_qkv.reshape(rows, 3, 8, 2, HEAD), ((0, 0),) * 4 + ((0, LANES - HEAD),))
    heads = heads.at[0, 1, :, :, HEAD : HEAD + 8].set(listed.astype(jnp.bfloat16)[None, None, :])
    heads = jnp.transpose(heads, (3, 2, 0, 1, 4)).reshape(2, 8, rows, 3 * LANES)
    embed = jnp.transpose(w_embed.reshape(rows, 2, -1), (1, 0, 2))[:, None]
    out = jnp.stack([w_out[:, :768], w_out[:, 640:]])[:, None]
    spread = lambda a: jnp.broadcast_to(a, (2, 8) + a.shape[2:])
    return jnp.concatenate([heads, spread(embed), spread(out)], axis=-1).reshape(16, rows, -1)


def pack_text(w_qkv, w_out):
    rows = w_qkv.shape[0]
    halves = jnp.concatenate(
        [
            jnp.transpose(w_qkv.reshape(rows, 3, 2, 512), (2, 0, 1, 3)).reshape(2, rows, 1536),
            jnp.transpose(w_out.reshape(rows, 2, 512), (1, 0, 2)),
        ],
        axis=-1,
    )
    return jnp.broadcast_to(halves[:, None], (2, 8, rows, 2048)).reshape(16 * rows, 2048)


def per_device(
    video_tokens,
    text_tokens,
    block_lists,
    positive_text,
    video_gain,
    w_video_qkv,
    w_video_out,
    text_gain,
    w_text_qkv,
    w_text_out,
    w_embed,
    gem_power,
    log_scale,
    logit_bias,
):
    h, c = lax.axis_index("h"), lax.axis_index("c")
    y, l = lax.axis_index("y"), lax.axis_index("l")
    t = 2 * y + l
    flat = video_tokens[0]

    normed = norm_rows(flat, video_gain)
    up = [(i, (i + 1) % 4) for i in range(4)]
    down = [(i, (i - 1) % 4) for i in range(4)]
    own_m = lax.ppermute(normed, "y", up)
    own_p = lax.ppermute(normed, "y", down)
    par = swap(normed, "l")
    par_m = lax.ppermute(par, "y", up)
    par_p = lax.ppermute(par, "y", down)
    own_o = lax.ppermute(own_m, "y", up)
    par_o = lax.ppermute(par_p, "y", down)
    arrived = [normed, own_m, own_p, par, par_m, par_p, own_o, par_o]
    turn = lambda dy, other: 2 * ((y + dy) % 4) + (1 - l if other else l)
    slots = jnp.stack(
        [turn(0, 0), turn(3, 0), turn(1, 0), turn(0, 1), turn(3, 1), turn(1, 1), turn(2, 0), turn(2, 1)]
    ).astype(jnp.int32)

    video = lax.all_to_all(pack_video(w_video_qkv, w_video_out, w_embed, block_lists[0, 0]), PLANE, 0, 0)
    lists = video[:, 0, LANES + HEAD : LANES + HEAD + 8].reshape(2, 8, 8)
    lists = jnp.where(c == 0, lists[0], lists[1]).astype(jnp.int32)
    video = video.reshape(-1, video.shape[-1])
    w_heads = video[:, : 3 * LANES]
    w_rest = video[:, 3 * LANES :]
    w_heads = ordered_pair(w_heads, swap(w_heads, "h"), h)
    w_heads = lax.all_gather(w_heads, "x", axis=0, tiled=True)
    text = lax.all_to_all(pack_text(w_text_qkv, w_text_out), PLANE, 0, 0, tiled=True)
    text = ordered_pair(text, swap(text, "h"), h)
    text = lax.all_gather(text, "x", axis=0, tiled=True)
    text_other = swap(text, "c")
    w_rest = ordered_pair(w_rest, swap(w_rest, "h"), h)
    w_rest = lax.all_gather(w_rest, "x", axis=0, tiled=True)
    rest_other = swap(w_rest, "c")
    heads_other = swap(w_heads, "c")
    w_heads = jnp.concatenate(
        [jnp.where(c == 0, w_heads, heads_other), jnp.where(c == 0, heads_other, w_heads)], axis=1
    )

    core = c.astype(jnp.int32)[None]
    blocks = [dot(block, w_heads).astype(jnp.bfloat16) for block in arrived]
    mixed = video_attend(lists, slots, blocks)

    texts, length, twidth = text_tokens.shape
    text_embed = text_layer(
        core, text_tokens.reshape(texts * length, twidth), text_gain[None], text, text_other
    )
    all_texts = lax.all_gather(text_embed, DP, axis=0, tiled=True)

    mixed = lax.all_to_all(mixed, TM, 0, 0)
    video_out, sums = video_project(core, gem_power, mixed, flat, w_rest, rest_other)
    sums = lax.all_to_all(sums, TM, 0, 0, tiled=True)
    ints = jnp.stack([c, t, positive_text[0]]).astype(jnp.int32)
    floats = jnp.stack([1.0 / gem_power[0], jnp.exp(log_scale[0]), logit_bias[0]])
    video_embed, part = pooled_loss(ints, floats, sums, w_rest, rest_other, all_texts, 8 * flat.shape[0])
    parts = lax.all_to_all(part, TM, 0, 0, tiled=True)
    clip_loss = jnp.sum(parts[:, 0])[None] / 128.0
    return (video_out[None], video_embed, text_embed, clip_loss)


def solution(mesh):
    fine = Mesh(mesh.devices.reshape(4, 2, 2, 4, 2), AXES)
    everywhere = P(DP + TM, None)
    return jax.shard_map(
        per_device,
        mesh=fine,
        in_specs=(
            P(DP, TM, None),
            P(DP + TM, None, None),
            P(DP, TM, None),
            P(DP),
            P(),
            everywhere,
            everywhere,
            P(),
            everywhere,
            everywhere,
            everywhere,
            P(),
            P(),
            P(),
        ),
        out_specs=(P(DP, TM, None), P(DP, None), everywhere, P(DP)),
        check_vma=False,
    )
```

```python
import functools

import jax
import jax.numpy as jnp
from jax import lax
from jax.experimental import pallas as pl
from jax.experimental.pallas import tpu as pltpu
from jax.sharding import Mesh
from jax.sharding import PartitionSpec as P

VHEADS = 16
THEADS = 16
HEAD = 88
LANES = 128
PIECE = 48
LOG2E = 1.4426950408889634

AXES = ("x", "h", "c", "y", "l")
DP = ("x", "h", "c")
TM = ("y", "l")
PLANE = ("h", "c", "y", "l")


def norm_rows(values, gain):
    full = values.astype(jnp.float32)
    scale = lax.rsqrt(jnp.mean(full * full, axis=-1, keepdims=True) + 1e-06)
    return (full * scale * gain).astype(jnp.bfloat16)


def swap(value, axis):
    return lax.ppermute(value, axis, [(0, 1), (1, 0)])


def dot(a, b):
    return jnp.dot(a, b, preferred_element_type=jnp.float32)


def dot_t(a, b):
    return lax.dot_general(a, b, (((1,), (1,)), ((), ())), preferred_element_type=jnp.float32)


def video_attend_kernel(places, lists, *refs):
    blocks, own, other, out_ref = refs[:8], refs[8:12], refs[12:16], refs[16]
    x, w, qk, vt, pairs, scores, tops, totals, accs, sems = refs[17:]
    rows = x.shape[1]
    depth = own[0].shape[0]
    wide = 3 * LANES
    core = places[12]
    copies = []
    for k in range(4):
        to = pl.ds(pl.multiple_of(depth * places[8 + k], 16), depth)
        for side, piece in ((core, own[k]), (1 - core, other[k])):
            lanes = pl.ds(pl.multiple_of(wide * side, LANES), wide)
            copies.append((piece.at[:, pl.ds(0, wide)], w.at[to, lanes]))
    for j in range(8):
        copies.append((blocks[j], x.at[j]))
    copies = [pltpu.make_async_copy(a, b, sems.at[n]) for n, (a, b) in enumerate(copies)]
    for copy in copies:
        copy.start()

    count = jnp.int32(0)
    for i in range(8):
        for k in range(8):
            pairs[0, count] = jnp.int32(i)
            pairs[1, count] = lists[i, k]
            pairs[2, count] = jnp.int32(k == 0)
            count = count + jnp.where(lists[i, k] >= 0, 1, 0)

    for copy in copies[:8]:
        copy.wait()
    for j in range(8):
        copies[8 + j].wait()
        qkv = dot(x[j], w[...])
        at = places[j]
        for head in range(2):
            cols = wide * head
            qk[at, :, 2 * LANES * head : 2 * LANES * (head + 1)] = qkv[:, cols : cols + 2 * LANES].astype(jnp.bfloat16)
            vt[at, head] = qkv[:, cols + 2 * LANES : cols + wide].T.astype(jnp.bfloat16)

    factor = jnp.float32(LOG2E / HEAD**0.5)

    def score(i, j, head):
        at = 2 * LANES * head
        return dot_t(qk[j, :, at + LANES : at + 2 * LANES], qk[i, :, at : at + LANES])

    for head in range(2):
        scores[0, head] = score(pairs[0, 0], pairs[1, 0], head)

    def one_pair(e, carry):
        slot = lax.rem(e, 2)
        i, j, first = pairs[0, e], pairs[1, e], pairs[2, e] == 1
        later = jnp.minimum(e + 1, count - 1)
        next_i, next_j = pairs[0, later], pairs[1, later]
        for head in range(2):
            ahead = score(next_i, next_j, head)
            s = scores[slot, head]
            top = jnp.where(first, jnp.full((1, rows), -1e30, jnp.float32), tops[head])
            top_new = jnp.maximum(top, jnp.max(s, axis=0, keepdims=True))
            shift = top_new * factor
            weights = jnp.exp2(s * factor - shift)
            old = jnp.exp2(top * factor - shift)
            tops[head] = top_new
            totals[head] = jnp.where(first, 0.0, totals[head]) * old + jnp.sum(weights, axis=0, keepdims=True)
            accs[head] = jnp.where(first, 0.0, accs[head]) * old + dot(vt[j, head], weights.astype(jnp.bfloat16))
            scores[1 - slot, head] = ahead

        @pl.when((e == count - 1) | (next_i != i))
        def _():
            for head in range(2):
                mixed = (accs[head] / totals[head]).astype(jnp.bfloat16)
                for l in range(2):
                    to = 2 * PIECE * l + PIECE * head
                    out_ref[i, to : to + PIECE] = mixed[PIECE * l : PIECE * (l + 1)]

        return carry

    lax.fori_loop(0, count, one_pair, 0)


def video_attend(places, lists, blocks, own, other):
    rows, width = blocks[0].shape
    smem = pl.BlockSpec(memory_space=pltpu.SMEM)
    hbm = pl.BlockSpec(memory_space=pl.ANY)
    return pl.pallas_call(
        video_attend_kernel,
        out_shape=jax.ShapeDtypeStruct((8, 4 * PIECE, rows), jnp.bfloat16),
        in_specs=[smem, smem] + [hbm] * 16,
        out_specs=pl.BlockSpec(memory_space=pltpu.VMEM),
        scratch_shapes=[
            pltpu.VMEM((8, rows, width), jnp.bfloat16),
            pltpu.VMEM((width, 6 * LANES), jnp.bfloat16),
            pltpu.VMEM((8, rows, 4 * LANES), jnp.bfloat16),
            pltpu.VMEM((8, 2, LANES, rows), jnp.bfloat16),
            pltpu.SMEM((3, 72), jnp.int32),
            pltpu.VMEM((2, 2, rows, rows), jnp.float32),
            pltpu.VMEM((2, 1, rows), jnp.float32),
            pltpu.VMEM((2, 1, rows), jnp.float32),
            pltpu.VMEM((2, LANES, rows), jnp.float32),
            pltpu.SemaphoreType.DMA((16,)),
        ],
        compiler_params=pltpu.CompilerParams(vmem_limit_bytes=48 * 2**20),
        cost_estimate=pl.CostEstimate(flops=9 * 10**9, bytes_accessed=10**7, transcendentals=5 * 10**6),
        name="video_attend",
    )(places, lists, *blocks, *own, *other)


def video_out_kernel(core, power, mixed, tokens, own, other, out_ref, sums_ref, w, sems):
    c = core[0]
    first = pltpu.make_async_copy(own, w.at[c], sems.at[0])
    second = pltpu.make_async_copy(other, w.at[1 - c], sems.at[1])
    first.start()
    second.start()
    first.wait()
    second.wait()
    p = power[0]
    for half, (low, high, skip) in enumerate(((0, 768, 0), (768, 1408, 128))):
        acc = tokens[:, low:high].astype(jnp.float32)
        total = jnp.zeros_like(acc)
        for t in range(8):
            total = total + lax.dot_general(
                mixed[t],
                w[half, 4 * PIECE * t : 4 * PIECE * (t + 1), skip:],
                (((0,), (0,)), ((), ())),
                preferred_element_type=jnp.float32,
            )
        out = (acc + total).astype(jnp.bfloat16)
        out_ref[:, low:high] = out
        grown = jnp.exp2(jnp.log2(jnp.maximum(out.astype(jnp.float32), 1e-06)) * p)
        sums_ref[:, low:high] = jnp.broadcast_to(jnp.sum(grown, axis=0, keepdims=True), (8, high - low))


def video_project(core, power, mixed, tokens, own, other):
    rows, width = tokens.shape
    vmem = pl.BlockSpec(memory_space=pltpu.VMEM)
    smem = pl.BlockSpec(memory_space=pltpu.SMEM)
    hbm = pl.BlockSpec(memory_space=pl.ANY)
    return pl.pallas_call(
        video_out_kernel,
        out_shape=(
            jax.ShapeDtypeStruct((rows, width), jnp.bfloat16),
            jax.ShapeDtypeStruct((8, width), jnp.float32),
        ),
        in_specs=[smem, smem, vmem, vmem, hbm, hbm],
        out_specs=(vmem, vmem),
        scratch_shapes=[pltpu.VMEM((2,) + own.shape, jnp.bfloat16), pltpu.SemaphoreType.DMA((2,))],
        compiler_params=pltpu.CompilerParams(vmem_limit_bytes=40 * 2**20),
        cost_estimate=pl.CostEstimate(flops=10**9, bytes_accessed=10**7, transcendentals=10**6),
        name="video_out",
    )(core, power, mixed, tokens, own, other)


def in_weight_order(rows):
    source = lax.broadcasted_iota(jnp.int32, (LANES, LANES), 0)
    to = lax.broadcasted_iota(jnp.int32, (LANES, LANES), 1)
    wanted = (source // 8) % 2 * 64 + source // 16 * 8 + source % 8
    order = jnp.where(to == wanted, 1.0, 0.0).astype(jnp.bfloat16)
    parts = [dot(rows[:, at : at + LANES], order).astype(jnp.bfloat16) for at in range(0, rows.shape[1], LANES)]
    return jnp.concatenate(parts, axis=1)


def text_kernel(core, tokens_ref, gain_ref, own, other, embed_ref, w, mixed, sems):
    c = core[0]

    @pl.when(pl.program_id(0) == 0)
    def _():
        first = pltpu.make_async_copy(own, w.at[c], sems.at[0])
        second = pltpu.make_async_copy(other, w.at[1 - c], sems.at[1])
        first.start()
        second.start()
        first.wait()
        second.wait()

    rows, width = tokens_ref.shape
    half = width // 2
    length = 64
    tokens = tokens_ref[...].astype(jnp.float32)
    scale = lax.rsqrt(jnp.mean(tokens * tokens, axis=-1, keepdims=True) + 1e-06)
    normed = in_weight_order((tokens * scale * gain_ref[...]).astype(jnp.bfloat16))
    same = (lax.broadcasted_iota(jnp.int32, (rows, rows), 0) // length) == (
        lax.broadcasted_iota(jnp.int32, (rows, rows), 1) // length
    )
    low = lax.broadcasted_iota(jnp.int32, (rows, LANES), 1) < length
    factor = jnp.float32(LOG2E / 8.0)
    for side in range(2):
        qkv = dot(normed, w[side, :, : 3 * half]).astype(jnp.bfloat16)
        for pair in range(half // LANES):
            at = pair * LANES
            q = qkv[:, at : at + LANES]
            key = qkv[:, half + at : half + at + LANES]
            value = qkv[:, 2 * half + at : 2 * half + at + LANES]
            outs = []
            for head in range(2):
                mine = low if head == 0 else jnp.logical_not(low)
                s = dot_t(jnp.where(mine, q, jnp.zeros_like(q)), key)
                s = jnp.where(same, s, jnp.float32(-1e30))
                top = jnp.max(s, axis=1, keepdims=True)
                weights = jnp.exp2((s - top) * factor)
                total = jnp.sum(weights, axis=1, keepdims=True)
                outs.append(dot(weights.astype(jnp.bfloat16), value) / total)
            o = jnp.where(low, outs[0], outs[1])
            mixed[:, side * half + at : side * half + at + LANES] = o.astype(jnp.bfloat16)
    whole = in_weight_order(mixed[...])
    means = []
    square = jnp.zeros((rows // length, 1), jnp.float32)
    for side in range(2):
        cols = slice(side * half, (side + 1) * half)
        projected = dot(whole, w[side, :, 3 * half :])
        out = (tokens_ref[:, cols].astype(jnp.float32) + projected).astype(jnp.bfloat16).astype(jnp.float32)
        mean = jnp.sum(out.reshape(rows // length, length, half), axis=1) * (1.0 / length)
        square = square + jnp.sum(mean * mean, axis=1, keepdims=True)
        means.append(mean)
    inverse = lax.rsqrt(square + 1e-06)
    for side in range(2):
        embed_ref[0, :, side * half : (side + 1) * half] = means[side] * inverse


def text_layer(core, tokens, gain, own, other):
    rows, width = tokens.shape
    step = 256
    smem = pl.BlockSpec(memory_space=pltpu.SMEM)
    hbm = pl.BlockSpec(memory_space=pl.ANY)
    out = pl.pallas_call(
        text_kernel,
        grid=(rows // step,),
        out_shape=jax.ShapeDtypeStruct((rows // step, step // 64, width), jnp.float32),
        in_specs=[
            smem,
            pl.BlockSpec((step, width), lambda i: (i, 0)),
            pl.BlockSpec((1, width), lambda i: (0, 0)),
            hbm,
            hbm,
        ],
        out_specs=pl.BlockSpec((1, step // 64, width), lambda i: (i, 0, 0)),
        scratch_shapes=[
            pltpu.VMEM((2,) + own.shape, jnp.bfloat16),
            pltpu.VMEM((step, width), jnp.bfloat16),
            pltpu.SemaphoreType.DMA((2,)),
        ],
        compiler_params=pltpu.CompilerParams(
            vmem_limit_bytes=48 * 2**20, dimension_semantics=("arbitrary",)
        ),
        cost_estimate=pl.CostEstimate(flops=17 * 10**9, bytes_accessed=10**7, transcendentals=4 * 10**6),
        name="text_layer",
    )(core, tokens, gain, own, other)
    return out.reshape(rows // 64, width)


def logits_kernel(places, floats, sums, texts, *refs, tokens):
    pieces, out_ref, columns, sems = refs[:4], refs[4], refs[5], refs[6]
    depth = pieces[0].shape[0]
    copies = []
    for k in range(4):
        to = pl.ds(pl.multiple_of(depth * places[8 + k], 16), depth)
        copies.append(pltpu.make_async_copy(pieces[k].at[:, pl.ds(3 * LANES, LANES)], columns.at[to], sems.at[k]))
    for copy in copies:
        copy.start()
    total = jnp.sum(sums[...], axis=0, keepdims=True)
    pooled = jnp.exp(jnp.log(total * (1.0 / tokens)) * floats[0]).astype(jnp.bfloat16)
    for copy in copies:
        copy.wait()
    proj = dot(jnp.broadcast_to(pooled, (16, pooled.shape[1])), columns[...])[:8]
    count = texts.shape[0]
    out_ref[:, :count] = lax.dot_general(
        proj,
        texts[...].astype(jnp.float32),
        (((1,), (1,)), ((), ())),
        precision=lax.Precision.HIGHEST,
        preferred_element_type=jnp.float32,
    )
    out_ref[:, count:] = proj


def partial_logits(places, floats, sums, texts, pieces, tokens):
    smem = pl.BlockSpec(memory_space=pltpu.SMEM)
    vmem = pl.BlockSpec(memory_space=pltpu.VMEM)
    return pl.pallas_call(
        functools.partial(logits_kernel, tokens=tokens),
        out_shape=jax.ShapeDtypeStruct((8, texts.shape[0] + LANES), jnp.float32),
        in_specs=[smem, smem, vmem, vmem] + [pl.BlockSpec(memory_space=pl.ANY)] * 4,
        out_specs=vmem,
        scratch_shapes=[pltpu.VMEM((sums.shape[1], LANES), jnp.bfloat16), pltpu.SemaphoreType.DMA((4,))],
        compiler_params=pltpu.CompilerParams(vmem_limit_bytes=32 * 2**20),
        cost_estimate=pl.CostEstimate(flops=10**7, bytes_accessed=10**6, transcendentals=10**4),
        name="partial_logits",
    )(places, floats, sums, texts, *pieces)


def loss_kernel(positive, floats, parts, embed_ref, loss_ref):
    count = parts.shape[1] - LANES
    proj = parts[:, count:]
    inverse = lax.rsqrt(jnp.sum(proj * proj, keepdims=True) + 1e-06)
    for t in range(8):
        embed_ref[:, LANES * t : LANES * (t + 1)] = proj[t : t + 1] * inverse
    raw = jnp.sum(parts[:, :count], axis=0, keepdims=True)
    logits = raw * (inverse * jnp.exp(jnp.full((1, 1), floats[1]))) + floats[2]
    ids = lax.broadcasted_iota(jnp.int32, (1, count), 1)
    z = jnp.where(ids == positive[0], -logits, logits)
    terms = jnp.maximum(z, 0.0) + jnp.log1p(jnp.exp(-jnp.abs(z)))
    loss_ref[...] = jnp.sum(terms, axis=1, keepdims=True) * (1.0 / 128.0)


def embed_and_loss(positive, floats, parts):
    smem = pl.BlockSpec(memory_space=pltpu.SMEM)
    vmem = pl.BlockSpec(memory_space=pltpu.VMEM)
    return pl.pallas_call(
        loss_kernel,
        out_shape=(
            jax.ShapeDtypeStruct((1, 8 * LANES), jnp.float32),
            jax.ShapeDtypeStruct((1, 1), jnp.float32),
        ),
        in_specs=[smem, smem, vmem],
        out_specs=(vmem, vmem),
        cost_estimate=pl.CostEstimate(flops=10**6, bytes_accessed=10**5, transcendentals=10**4),
        name="embed_and_loss",
    )(positive, floats, parts)


def pack_kernel(listed, w_heads, w_out, w_embed, w_text, w_text_out, shared_ref, columns_ref):
    rows = w_heads.shape[0]
    lane = lax.broadcasted_iota(jnp.int32, (rows, LANES), 1)
    row = lax.broadcasted_iota(jnp.int32, (rows, LANES), 0)
    half = w_text_out.shape[1] // 2
    width = w_heads.shape[1] // 3
    pad = jnp.zeros((rows, LANES - HEAD), jnp.float32)
    carried = (row == 0) & (lane >= HEAD) & (lane < HEAD + 8)
    source = lax.broadcasted_iota(jnp.int32, (HEAD, LANES), 0)
    to_lane = lax.broadcasted_iota(jnp.int32, (HEAD, LANES), 1)
    wanted = (source // 11) % 2 * PIECE + source // 22 * 11 + source % 11
    order = jnp.where(to_lane == wanted, 1.0, 0.0).astype(jnp.bfloat16)
    shared_ref[...] = jnp.zeros_like(shared_ref)
    for c in range(2):
        piece = lambda i: w_text[:, 2 * half * i + half * c : 2 * half * i + half * (c + 1)].astype(jnp.float32)
        upper = jnp.concatenate([piece(0), piece(1)], axis=1)
        lower = jnp.concatenate([piece(2), w_text_out[:, half * c : half * (c + 1)].astype(jnp.float32)], axis=1)
        text = jnp.concatenate([upper, lower], axis=0).astype(jnp.bfloat16)
        for y in range(4):
            shared_ref[4 * c + y, :, :1024] = text
            shared_ref[4 * c + y, :rows, 1024:] = w_out[:, 640 * c : 640 * c + 768]
        for t in range(8):
            head = 2 * t + c
            for part in range(3):
                at = width * part + HEAD * head
                value = w_heads[:, at : at + HEAD]
                if part == 2:
                    value = dot(value, order)
                else:
                    value = jnp.concatenate([value.astype(jnp.float32), pad], axis=1)
                if part == 1:
                    value = jnp.where(carried, listed[...], value)
                for h in range(2):
                    columns_ref[16 * h + 8 * c + t, :, LANES * part : LANES * (part + 1)] = value.astype(jnp.bfloat16)
            for h in range(2):
                columns_ref[16 * h + 8 * c + t, :, 3 * LANES :] = w_embed[:, LANES * t : LANES * (t + 1)]


def pack_weights(listed, w_heads, *weights):
    vmem = pl.BlockSpec(memory_space=pltpu.VMEM)
    rows = w_heads.shape[0]
    return pl.pallas_call(
        pack_kernel,
        out_shape=(
            jax.ShapeDtypeStruct((8, 16, 1792), jnp.bfloat16),
            jax.ShapeDtypeStruct((32, rows, 4 * LANES), jnp.bfloat16),
        ),
        in_specs=[vmem] * 6,
        out_specs=(vmem,) * 2,
        compiler_params=pltpu.CompilerParams(vmem_limit_bytes=32 * 2**20),
        cost_estimate=pl.CostEstimate(flops=10**6, bytes_accessed=3 * 10**6, transcendentals=0),
        name="pack_weights",
    )(listed, w_heads, *weights)


def per_device(
    video_tokens,
    text_tokens,
    block_lists,
    positive_text,
    video_gain,
    w_video_qkv,
    w_video_out,
    text_gain,
    w_text_qkv,
    w_text_out,
    w_embed,
    gem_power,
    log_scale,
    logit_bias,
):
    h, c = lax.axis_index("h"), lax.axis_index("c")
    y, l = lax.axis_index("y"), lax.axis_index("l")
    t = 2 * y + l
    flat = video_tokens[0]

    normed = norm_rows(flat, video_gain)
    up = [(i, (i + 1) % 4) for i in range(4)]
    down = [(i, (i - 1) % 4) for i in range(4)]
    own_m = lax.ppermute(normed, "y", up)
    own_p = lax.ppermute(normed, "y", down)
    par = swap(normed, "l")

    listed = jnp.pad(block_lists[0].astype(jnp.float32), ((0, 0), (HEAD, LANES - HEAD - 8)))
    shared, columns = pack_weights(listed, w_video_qkv, w_video_out, w_embed, w_text_qkv, w_text_out)
    shared = lax.all_to_all(shared, ("c", "y"), 0, 0)
    shared, columns, own_m, own_p, par = lax.optimization_barrier((shared, columns, own_m, own_p, par))
    own_o = lax.ppermute(own_m, "y", up)
    par_m = swap(own_m, "l")
    par_p = lax.ppermute(par, "y", down)

    text = jnp.transpose(shared[:, :, :1024].reshape(8, 2, 8, 1024), (0, 2, 1, 3)).reshape(64, 2048)
    w_out = jnp.pad(shared[:, :11, 1024:].reshape(2, 44, 768), ((0, 0), (0, PIECE - 44), (0, 0))).reshape(-1, 768)
    text = lax.all_gather(text, ("x", "h", "l"), axis=0, tiled=True)
    w_out = lax.all_gather(w_out, ("x", "h", "l"), axis=0, tiled=True)

    columns = lax.all_to_all(columns, PLANE, 0, 0)
    columns, own_o, par_m, par_p = lax.optimization_barrier((columns, own_o, par_m, par_p))
    par_o = lax.ppermute(par_p, "y", down)
    lists = columns[:, 0, LANES + HEAD : LANES + HEAD + 8].reshape(4, 8, 8)
    lists = lax.dynamic_index_in_dim(lists, 2 * h + c, 0, keepdims=False).astype(jnp.int32)
    columns = columns.reshape(-1, columns.shape[-1])
    x = lax.axis_index("x")
    pieces = [columns] + [lax.ppermute(columns, "x", [(i, (i - k) % 4) for i in range(4)]) for k in (1, 2, 3)]
    pieces_other = [swap(columns, "c")]
    *pieces[1:], par_o, pieces_other[0] = lax.optimization_barrier((*pieces[1:], par_o, pieces_other[0]))
    pieces_other += [swap(piece, "c") for piece in pieces[1:]]

    arrived = [normed, own_m, own_p, par, par_m, par_p, own_o, par_o]
    turn = lambda dy, other: 2 * ((y + dy) % 4) + (1 - l if other else l)
    turns = [turn(0, 0), turn(3, 0), turn(1, 0), turn(0, 1), turn(3, 1), turn(1, 1), turn(2, 0), turn(2, 1)]
    places = jnp.stack(turns + [(x + k) % 4 for k in range(4)] + [c]).astype(jnp.int32)
    mixed = video_attend(places, lists, arrived, pieces, pieces_other)

    core = c.astype(jnp.int32)[None]
    text, *pieces_other = lax.optimization_barrier((text, *pieces_other))
    text_other = swap(text, "c")
    mixed, tokens = lax.optimization_barrier((mixed, text_tokens))
    mixed = lax.all_to_all(mixed, TM, 0, 0)

    texts, length, twidth = text_tokens.shape
    text_embed = text_layer(
        core, tokens.reshape(texts * length, twidth), text_gain[None], text, text_other
    )
    sent = jnp.transpose(text_embed.astype(jnp.bfloat16).reshape(texts, 8, LANES), (1, 0, 2))
    sent = jnp.broadcast_to(sent[None], (16,) + sent.shape).reshape(128, texts, LANES)
    sent, w_out = lax.optimization_barrier((sent, w_out))
    out_other = swap(w_out, "c")
    all_texts = lax.all_to_all(sent, AXES, 0, 0).reshape(128 * texts, LANES)
    mixed, sent = lax.optimization_barrier((mixed, sent))

    video_out, sums = video_project(core, gem_power, mixed, flat, w_out, out_other)
    sums, all_texts = lax.optimization_barrier((sums, all_texts))
    sums = lax.all_to_all(sums, TM, 0, 0, tiled=True)
    floats = jnp.stack([1.0 / gem_power[0], log_scale[0], logit_bias[0]])
    parts = partial_logits(places, floats, sums, all_texts, pieces, 8 * flat.shape[0])
    parts = lax.all_to_all(parts, TM, 0, 0, tiled=True)
    video_embed, clip_loss = embed_and_loss(positive_text, floats, parts)
    return (video_out[None], video_embed, text_embed, clip_loss[0])


def solution(mesh):
    fine = Mesh(mesh.devices.reshape(4, 2, 2, 4, 2), AXES)
    everywhere = P(DP + TM, None)
    return jax.shard_map(
        per_device,
        mesh=fine,
        in_specs=(
            P(DP, TM, None),
            P(DP + TM, None, None),
            P(DP, TM, None),
            P(DP),
            P(),
            everywhere,
            everywhere,
            P(),
            everywhere,
            everywhere,
            everywhere,
            P(),
            P(),
            P(),
        ),
        out_specs=(P(DP, TM, None), P(DP, None), everywhere, P(DP)),
        check_vma=False,
    )
```

```python
import functools

import jax
import jax.numpy as jnp
from jax import lax
from jax.experimental import pallas as pl
from jax.experimental.pallas import tpu as pltpu
from jax.sharding import Mesh
from jax.sharding import PartitionSpec as P

VHEADS = 16
THEADS = 16
HEAD = 88
LANES = 128
PIECE = 48
LOG2E = 1.4426950408889634

AXES = ("x", "h", "c", "y", "l")
DP = ("x", "h", "c")
TM = ("y", "l")
PLANE = ("h", "c", "y", "l")


def norm_rows(values, gain):
    full = values.astype(jnp.float32)
    scale = lax.rsqrt(jnp.mean(full * full, axis=-1, keepdims=True) + 1e-06)
    return (full * scale * gain).astype(jnp.bfloat16)


def swap(value, axis):
    return lax.ppermute(value, axis, [(0, 1), (1, 0)])


def dot(a, b):
    return jnp.dot(a, b, preferred_element_type=jnp.float32)


def dot_t(a, b):
    return lax.dot_general(a, b, (((1,), (1,)), ((), ())), preferred_element_type=jnp.float32)


def video_qkv_kernel(places, *refs):
    blocks, own, other, qk_ref, vt_ref, x, w, sems = refs[:9], *refs[9:]
    wide = 3 * LANES
    core = places[8]
    copies = []
    for side, columns in ((core, own), (1 - core, other)):
        copies.append((columns, w.at[:, pl.ds(pl.multiple_of(wide * side, LANES), wide)]))
    half = x.shape[1] // 2
    for j in range(7):
        copies.append((blocks[j], x.at[j]))
    for n in range(2):
        copies.append((blocks[7 + n], x.at[7, pl.ds(half * n, half)]))
    copies = [pltpu.make_async_copy(a, b, sems.at[n]) for n, (a, b) in enumerate(copies)]
    for copy in copies:
        copy.start()
    for copy in copies[:2]:
        copy.wait()
    for copy in copies[2:]:
        copy.wait()
    rows = x.shape[1]
    whole = dot(x[...].reshape(8 * rows, x.shape[2]), w[...])
    for j in range(8):
        qkv = whole[rows * j : rows * (j + 1)]
        at = places[j]
        for head in range(2):
            cols = wide * head
            qk_ref[at, :, 2 * LANES * head : 2 * LANES * (head + 1)] = qkv[:, cols : cols + 2 * LANES].astype(
                jnp.bfloat16
            )
            vt_ref[at, head] = qkv[:, cols + 2 * LANES : cols + wide].T.astype(jnp.bfloat16)


def video_qkv(places, blocks, own, other):
    rows, width = blocks[0].shape
    vmem = pl.BlockSpec(memory_space=pltpu.VMEM)
    return pl.pallas_call(
        video_qkv_kernel,
        out_shape=(
            jax.ShapeDtypeStruct((8, rows, 4 * LANES), jnp.bfloat16),
            jax.ShapeDtypeStruct((8, 2, LANES, rows), jnp.bfloat16),
        ),
        in_specs=[pl.BlockSpec(memory_space=pltpu.SMEM)] + [pl.BlockSpec(memory_space=pl.ANY)] * 11,
        out_specs=(vmem, vmem),
        scratch_shapes=[
            pltpu.VMEM((8, rows, width), jnp.bfloat16),
            pltpu.VMEM((width, 6 * LANES), jnp.bfloat16),
            pltpu.SemaphoreType.DMA((11,)),
        ],
        compiler_params=pltpu.CompilerParams(vmem_limit_bytes=50 * 2**20),
        cost_estimate=pl.CostEstimate(flops=5 * 10**9, bytes_accessed=10**7, transcendentals=0),
        name="video_qkv",
    )(places, *blocks, own, other)


def video_attend_kernel(lists, qk, vt, out_ref, pairs, scores, tops, totals, accs):
    rows = qk.shape[1]
    count = jnp.int32(0)
    for i in range(8):
        for k in range(8):
            pairs[0, count] = jnp.int32(i)
            pairs[1, count] = lists[i, k]
            pairs[2, count] = jnp.int32(k == 0)
            count = count + jnp.where(lists[i, k] >= 0, 1, 0)

    factor = jnp.float32(LOG2E / HEAD**0.5)

    def score(i, j, head):
        at = 2 * LANES * head
        return dot_t(qk[j, :, at + LANES : at + 2 * LANES], qk[i, :, at : at + LANES])

    for head in range(2):
        scores[0, head] = score(pairs[0, 0], pairs[1, 0], head)

    def one_pair(e, carry):
        slot = lax.rem(e, 2)
        i, j, first = pairs[0, e], pairs[1, e], pairs[2, e] == 1
        later = jnp.minimum(e + 1, count - 1)
        next_i, next_j = pairs[0, later], pairs[1, later]
        for head in range(2):
            ahead = score(next_i, next_j, head)
            s = scores[slot, head]
            top = jnp.where(first, jnp.full((1, rows), -1e30, jnp.float32), tops[head])
            top_new = jnp.maximum(top, jnp.max(s, axis=0, keepdims=True))
            shift = top_new * factor
            weights = jnp.exp2(s * factor - shift)
            old = jnp.exp2(top * factor - shift)
            tops[head] = top_new
            totals[head] = jnp.where(first, 0.0, totals[head]) * old + jnp.sum(weights, axis=0, keepdims=True)
            accs[head] = jnp.where(first, 0.0, accs[head]) * old + dot(vt[j, head], weights.astype(jnp.bfloat16))
            scores[1 - slot, head] = ahead

        @pl.when((e == count - 1) | (next_i != i))
        def _():
            for head in range(2):
                mixed = (accs[head] / totals[head]).astype(jnp.bfloat16)
                for l in range(2):
                    to = 2 * PIECE * l + PIECE * head
                    out_ref[i, to : to + PIECE] = mixed[PIECE * l : PIECE * (l + 1)]

        return carry

    lax.fori_loop(0, count, one_pair, 0)


def video_attend(lists, qk, vt):
    rows = qk.shape[1]
    vmem = pl.BlockSpec(memory_space=pltpu.VMEM)
    return pl.pallas_call(
        video_attend_kernel,
        out_shape=jax.ShapeDtypeStruct((8, 4 * PIECE, rows), jnp.bfloat16),
        in_specs=[pl.BlockSpec(memory_space=pltpu.SMEM), vmem, vmem],
        out_specs=vmem,
        scratch_shapes=[
            pltpu.SMEM((3, 72), jnp.int32),
            pltpu.VMEM((2, 2, rows, rows), jnp.float32),
            pltpu.VMEM((2, 1, rows), jnp.float32),
            pltpu.VMEM((2, 1, rows), jnp.float32),
            pltpu.VMEM((2, LANES, rows), jnp.float32),
        ],
        compiler_params=pltpu.CompilerParams(vmem_limit_bytes=32 * 2**20),
        cost_estimate=pl.CostEstimate(flops=4 * 10**9, bytes_accessed=4 * 10**6, transcendentals=5 * 10**6),
        name="video_attend",
    )(lists, qk, vt)


def video_out_kernel(core, power, mixed, tokens, own, other, out_ref, sums_ref, w, sems):
    c = core[0]
    first = pltpu.make_async_copy(own, w.at[c], sems.at[0])
    second = pltpu.make_async_copy(other, w.at[1 - c], sems.at[1])
    first.start()
    second.start()
    first.wait()
    second.wait()
    p = power[0]
    for half, (low, high, skip) in enumerate(((0, 768, 0), (768, 1408, 128))):
        acc = tokens[:, low:high].astype(jnp.float32)
        total = jnp.zeros_like(acc)
        for t in range(8):
            total = total + lax.dot_general(
                mixed[t],
                w[half, 4 * PIECE * t : 4 * PIECE * (t + 1), skip:],
                (((0,), (0,)), ((), ())),
                preferred_element_type=jnp.float32,
            )
        out = (acc + total).astype(jnp.bfloat16)
        out_ref[:, low:high] = out
        grown = jnp.exp2(jnp.log2(jnp.maximum(out.astype(jnp.float32), 1e-06)) * p)
        sums_ref[:, low:high] = jnp.broadcast_to(jnp.sum(grown, axis=0, keepdims=True), (8, high - low))


def video_project(core, power, mixed, tokens, own, other):
    rows, width = tokens.shape
    vmem = pl.BlockSpec(memory_space=pltpu.VMEM)
    smem = pl.BlockSpec(memory_space=pltpu.SMEM)
    hbm = pl.BlockSpec(memory_space=pl.ANY)
    return pl.pallas_call(
        video_out_kernel,
        out_shape=(
            jax.ShapeDtypeStruct((rows, width), jnp.bfloat16),
            jax.ShapeDtypeStruct((8, width), jnp.float32),
        ),
        in_specs=[smem, smem, vmem, vmem, hbm, hbm],
        out_specs=(vmem, vmem),
        scratch_shapes=[pltpu.VMEM((2,) + own.shape, jnp.bfloat16), pltpu.SemaphoreType.DMA((2,))],
        compiler_params=pltpu.CompilerParams(vmem_limit_bytes=40 * 2**20),
        cost_estimate=pl.CostEstimate(flops=10**9, bytes_accessed=10**7, transcendentals=10**6),
        name="video_out",
    )(core, power, mixed, tokens, own, other)


def in_weight_order(rows):
    source = lax.broadcasted_iota(jnp.int32, (LANES, LANES), 0)
    to = lax.broadcasted_iota(jnp.int32, (LANES, LANES), 1)
    wanted = (source // 8) % 2 * 64 + source // 16 * 8 + source % 8
    order = jnp.where(to == wanted, 1.0, 0.0).astype(jnp.bfloat16)
    parts = [dot(rows[:, at : at + LANES], order).astype(jnp.bfloat16) for at in range(0, rows.shape[1], LANES)]
    return jnp.concatenate(parts, axis=1)


def text_kernel(core, tokens_ref, gain_ref, own, other, embed_ref, w, mixed, sems):
    c = core[0]
    sides = (c, 1 - c)
    copies = [pltpu.make_async_copy(part, w.at[side], sems.at[n]) for n, (part, side) in enumerate(zip((own, other), sides))]
    for copy in copies:
        copy.start()
    rows, width = tokens_ref.shape
    half = width // 2
    length = 64
    tile = 256
    tokens = tokens_ref[...].astype(jnp.float32)
    scale = lax.rsqrt(jnp.mean(tokens * tokens, axis=-1, keepdims=True) + 1e-06)
    normed = in_weight_order((tokens * scale * gain_ref[...]).astype(jnp.bfloat16))
    same = (lax.broadcasted_iota(jnp.int32, (2 * tile, tile), 0) % tile // length) == (
        lax.broadcasted_iota(jnp.int32, (2 * tile, tile), 1) // length
    )
    low = lax.broadcasted_iota(jnp.int32, (tile, LANES), 1) < length
    factor = jnp.float32(LOG2E / 8.0)
    for copy, side in zip(copies, sides):
        copy.wait()
        qkv = dot(normed, w[side, :, : 3 * half]).astype(jnp.bfloat16)
        for pair in range(half // LANES):
            at = pair * LANES
            to = pl.ds(pl.multiple_of(side * half + at, LANES), LANES)
            for sub in range(0, rows, tile):
                q = qkv[sub : sub + tile, at : at + LANES]
                key = qkv[sub : sub + tile, half + at : half + at + LANES]
                value = qkv[sub : sub + tile, 2 * half + at : 2 * half + at + LANES]
                none = jnp.zeros_like(q)
                s = dot_t(jnp.concatenate([jnp.where(low, q, none), jnp.where(low, none, q)], axis=0), key)
                s = jnp.where(same, s, jnp.float32(-1e30))
                top = jnp.max(s, axis=1, keepdims=True)
                weights = jnp.exp2((s - top) * factor)
                total = jnp.sum(weights, axis=1, keepdims=True)
                o = dot(weights.astype(jnp.bfloat16), value) / total
                mixed[sub : sub + tile, to] = jnp.where(low, o[:tile], o[tile:]).astype(jnp.bfloat16)
    whole = in_weight_order(mixed[...])
    means = []
    square = jnp.zeros((rows // length, 1), jnp.float32)
    for side in range(2):
        cols = slice(side * half, (side + 1) * half)
        projected = dot(whole, w[side, :, 3 * half :])
        out = (tokens_ref[:, cols].astype(jnp.float32) + projected).astype(jnp.bfloat16).astype(jnp.float32)
        mean = jnp.sum(out.reshape(rows // length, length, half), axis=1) * (1.0 / length)
        square = square + jnp.sum(mean * mean, axis=1, keepdims=True)
        means.append(mean)
    inverse = lax.rsqrt(square + 1e-06)
    for side in range(2):
        embed_ref[:, side * half : (side + 1) * half] = means[side] * inverse


def text_layer(core, tokens, gain, own, other):
    rows, width = tokens.shape
    vmem = pl.BlockSpec(memory_space=pltpu.VMEM)
    hbm = pl.BlockSpec(memory_space=pl.ANY)
    return pl.pallas_call(
        text_kernel,
        out_shape=jax.ShapeDtypeStruct((rows // 64, width), jnp.float32),
        in_specs=[pl.BlockSpec(memory_space=pltpu.SMEM), vmem, vmem, hbm, hbm],
        out_specs=vmem,
        scratch_shapes=[
            pltpu.VMEM((2,) + own.shape, jnp.bfloat16),
            pltpu.VMEM((rows, width), jnp.bfloat16),
            pltpu.SemaphoreType.DMA((2,)),
        ],
        compiler_params=pltpu.CompilerParams(vmem_limit_bytes=50 * 2**20),
        cost_estimate=pl.CostEstimate(flops=17 * 10**9, bytes_accessed=10**7, transcendentals=4 * 10**6),
        name="text_layer",
    )(core, tokens, gain, own, other)


def logits_kernel(floats, sums, texts, columns, out_ref, *, tokens):
    total = sums[0:1]
    pooled = jnp.exp(jnp.log(total * (1.0 / tokens)) * floats[0]).astype(jnp.bfloat16)
    proj = dot(jnp.broadcast_to(pooled, (16, pooled.shape[1])), columns[...])[:8]
    count = texts.shape[0]
    out_ref[:, :count] = lax.dot_general(
        proj,
        texts[...].astype(jnp.float32),
        (((1,), (1,)), ((), ())),
        precision=lax.Precision.HIGHEST,
        preferred_element_type=jnp.float32,
    )
    out_ref[:, count:] = proj


def partial_logits(floats, sums, texts, columns, tokens):
    smem = pl.BlockSpec(memory_space=pltpu.SMEM)
    vmem = pl.BlockSpec(memory_space=pltpu.VMEM)
    return pl.pallas_call(
        functools.partial(logits_kernel, tokens=tokens),
        out_shape=jax.ShapeDtypeStruct((8, texts.shape[0] + LANES), jnp.float32),
        in_specs=[smem, vmem, vmem, vmem],
        out_specs=vmem,
        compiler_params=pltpu.CompilerParams(vmem_limit_bytes=32 * 2**20),
        cost_estimate=pl.CostEstimate(flops=10**7, bytes_accessed=10**6, transcendentals=10**4),
        name="partial_logits",
    )(floats, sums, texts, columns)


def loss_kernel(positive, floats, parts, embed_ref, loss_ref):
    count = parts.shape[1] - LANES
    proj = parts[:, count:]
    inverse = lax.rsqrt(jnp.sum(proj * proj, keepdims=True) + 1e-06)
    for t in range(8):
        embed_ref[:, LANES * t : LANES * (t + 1)] = proj[t : t + 1] * inverse
    raw = jnp.sum(parts[:, :count], axis=0, keepdims=True)
    logits = raw * (inverse * jnp.exp(jnp.full((1, 1), floats[1]))) + floats[2]
    ids = lax.broadcasted_iota(jnp.int32, (1, count), 1)
    z = jnp.where(ids == positive[0], -logits, logits)
    terms = jnp.maximum(z, 0.0) + jnp.log1p(jnp.exp(-jnp.abs(z)))
    loss_ref[...] = jnp.sum(terms, axis=1, keepdims=True) * (1.0 / 128.0)


def embed_and_loss(positive, floats, parts):
    smem = pl.BlockSpec(memory_space=pltpu.SMEM)
    vmem = pl.BlockSpec(memory_space=pltpu.VMEM)
    return pl.pallas_call(
        loss_kernel,
        out_shape=(
            jax.ShapeDtypeStruct((1, 8 * LANES), jnp.float32),
            jax.ShapeDtypeStruct((1, 1), jnp.float32),
        ),
        in_specs=[smem, smem, vmem],
        out_specs=(vmem, vmem),
        cost_estimate=pl.CostEstimate(flops=10**6, bytes_accessed=10**5, transcendentals=10**4),
        name="embed_and_loss",
    )(positive, floats, parts)


def pack_kernel(listed, w_heads, w_out, w_embed, w_text, w_text_out, shared_ref, columns_ref, embed_ref):
    rows = w_heads.shape[0]
    lane = lax.broadcasted_iota(jnp.int32, (rows, LANES), 1)
    row = lax.broadcasted_iota(jnp.int32, (rows, LANES), 0)
    half = w_text_out.shape[1] // 2
    width = w_heads.shape[1] // 3
    pad = jnp.zeros((rows, LANES - HEAD), jnp.float32)
    carried = (row == 0) & (lane >= HEAD) & (lane < HEAD + 8)
    source = lax.broadcasted_iota(jnp.int32, (HEAD, LANES), 0)
    to_lane = lax.broadcasted_iota(jnp.int32, (HEAD, LANES), 1)
    wanted = (source // 11) % 2 * PIECE + source // 22 * 12 + source % 11
    order = jnp.where(to_lane == wanted, 1.0, 0.0).astype(jnp.bfloat16)
    shared_ref[...] = jnp.zeros_like(shared_ref)
    embed_ref[...] = jnp.zeros_like(embed_ref)
    for c in range(2):
        piece = lambda i: w_text[:, 2 * half * i + half * c : 2 * half * i + half * (c + 1)].astype(jnp.float32)
        upper = jnp.concatenate([piece(0), piece(1)], axis=1)
        lower = jnp.concatenate([piece(2), w_text_out[:, half * c : half * (c + 1)].astype(jnp.float32)], axis=1)
        text = jnp.concatenate([upper, lower], axis=0).astype(jnp.bfloat16)
        for y in range(4):
            shared_ref[4 * c + y, :, :1024] = text
            shared_ref[4 * c + y, :rows, 1024:] = w_out[:, 640 * c : 640 * c + 768]
        for t in range(8):
            head = 2 * t + c
            for part in range(3):
                at = width * part + HEAD * head
                value = w_heads[:, at : at + HEAD]
                if part == 2:
                    value = dot(value, order)
                else:
                    value = jnp.concatenate([value.astype(jnp.float32), pad], axis=1)
                if part == 1:
                    value = jnp.where(carried, listed[...], value)
                value = value.astype(jnp.bfloat16)
                for plane in range(8):
                    columns_ref[16 * plane + 8 * c + t, :, LANES * part : LANES * (part + 1)] = value
            for plane in range(8):
                embed_ref[16 * plane + 8 * c + t, :rows] = w_embed[:, LANES * t : LANES * (t + 1)]


def pack_weights(listed, w_heads, *weights):
    vmem = pl.BlockSpec(memory_space=pltpu.VMEM)
    rows = w_heads.shape[0]
    return pl.pallas_call(
        pack_kernel,
        out_shape=(
            jax.ShapeDtypeStruct((8, 16, 1792), jnp.bfloat16),
            jax.ShapeDtypeStruct((128, rows, 3 * LANES), jnp.bfloat16),
            jax.ShapeDtypeStruct((128, 16, LANES), jnp.bfloat16),
        ),
        in_specs=[vmem] * 6,
        out_specs=(vmem,) * 3,
        compiler_params=pltpu.CompilerParams(vmem_limit_bytes=32 * 2**20),
        cost_estimate=pl.CostEstimate(flops=10**6, bytes_accessed=3 * 10**6, transcendentals=0),
        name="pack_weights",
    )(listed, w_heads, *weights)


def per_device(
    video_tokens,
    text_tokens,
    block_lists,
    positive_text,
    video_gain,
    w_video_qkv,
    w_video_out,
    text_gain,
    w_text_qkv,
    w_text_out,
    w_embed,
    gem_power,
    log_scale,
    logit_bias,
):
    h, c = lax.axis_index("h"), lax.axis_index("c")
    y, l = lax.axis_index("y"), lax.axis_index("l")
    t = 2 * y + l
    flat = video_tokens[0]

    normed = norm_rows(flat, video_gain)
    up = [(i, (i + 1) % 4) for i in range(4)]
    down = [(i, (i - 1) % 4) for i in range(4)]
    own_m = lax.ppermute(normed, "y", up)
    own_p = lax.ppermute(normed, "y", down)
    par = swap(normed, "l")

    listed = jnp.pad(block_lists[0].astype(jnp.float32), ((0, 0), (HEAD, LANES - HEAD - 8)))
    shared, columns, embed = pack_weights(listed, w_video_qkv, w_video_out, w_embed, w_text_qkv, w_text_out)
    shared = lax.all_to_all(shared, ("c", "y"), 0, 0)
    shared, columns, own_m, own_p, par = lax.optimization_barrier((shared, columns, own_m, own_p, par))
    part = normed.shape[0] // 2
    own_o = lax.ppermute(own_m, "y", up)
    par_m = swap(own_m, "l")
    par_p = lax.ppermute(par, "y", down)
    par_o = [lax.ppermute(par_m[:part], "y", up), lax.ppermute(par_p[part:], "y", down)]

    text = jnp.transpose(shared[:, :, :1024].reshape(8, 2, 8, 1024), (0, 2, 1, 3)).reshape(64, 2048)
    w_out = shared[:, :12, 1024:].reshape(2 * PIECE, 768)
    text = lax.all_gather(text, ("x", "h", "l"), axis=0, tiled=True)

    columns = lax.all_to_all(columns, AXES, 0, 0)
    columns, own_o, par_m, par_p, par_o[0], par_o[1] = lax.optimization_barrier(
        (columns, own_o, par_m, par_p, par_o[0], par_o[1])
    )
    lists = columns[:, 0, LANES + HEAD : LANES + HEAD + 8].reshape(16, 8, 8)
    lists = lax.dynamic_index_in_dim(lists, 4 * lax.axis_index("x") + 2 * h + c, 0, keepdims=False)
    lists = lists.astype(jnp.int32)
    columns = columns.reshape(-1, columns.shape[-1])
    columns_other = swap(columns, "c")
    columns_other, w_out = lax.optimization_barrier((columns_other, w_out))
    w_out = lax.all_gather(w_out, ("x", "h", "l"), axis=0, tiled=True)
    arrived = [normed, own_m, own_p, par, par_m, par_p, own_o] + par_o
    turn = lambda dy, other: 2 * ((y + dy) % 4) + (1 - l if other else l)
    turns = [turn(0, 0), turn(3, 0), turn(1, 0), turn(0, 1), turn(3, 1), turn(1, 1), turn(2, 0), turn(2, 1)]
    places = jnp.stack(turns + [c]).astype(jnp.int32)
    qk, vt = video_qkv(places, arrived, columns, columns_other)
    text, qk, vt = lax.optimization_barrier((text, qk, vt))
    text_other = swap(text, "c")
    mixed = video_attend(lists, qk, vt)

    core = c.astype(jnp.int32)[None]
    mixed, tokens = lax.optimization_barrier((mixed, text_tokens))
    mixed = lax.all_to_all(mixed, TM, 0, 0)

    texts, length, twidth = text_tokens.shape
    text_embed = text_layer(
        core, tokens.reshape(texts * length, twidth), text_gain[None], text, text_other
    )
    mixed, text_embed, w_out = lax.optimization_barrier((mixed, text_embed, w_out))
    out_other = swap(w_out, "c")
    sent = jnp.transpose(text_embed.astype(jnp.bfloat16).reshape(texts, 8, LANES), (1, 0, 2))
    sent = jnp.broadcast_to(sent[None], (16,) + sent.shape).reshape(128, texts, LANES)
    sent = lax.all_to_all(jnp.concatenate([sent, embed], axis=1), AXES, 0, 0)
    all_texts = sent[:, :texts].reshape(128 * texts, LANES)
    embed = sent[:, texts : texts + w_embed.shape[0]].reshape(-1, LANES)

    video_out, sums = video_project(core, gem_power, mixed, flat, w_out, out_other)
    sums = sums + swap(sums, "l")
    sums = sums + sum(lax.ppermute(sums, "y", [(i, (i + k) % 4) for i in range(4)]) for k in (1, 2, 3))
    floats = jnp.stack([1.0 / gem_power[0], log_scale[0], logit_bias[0]])
    parts = partial_logits(floats, sums, all_texts, embed, 8 * flat.shape[0])
    parts = lax.all_to_all(parts, TM, 0, 0, tiled=True)
    video_embed, clip_loss = embed_and_loss(positive_text, floats, parts)
    return (video_out[None], video_embed, text_embed, clip_loss[0])


def solution(mesh):
    fine = Mesh(mesh.devices.reshape(4, 2, 2, 4, 2), AXES)
    everywhere = P(DP + TM, None)
    return jax.shard_map(
        per_device,
        mesh=fine,
        in_specs=(
            P(DP, TM, None),
            P(DP + TM, None, None),
            P(DP, TM, None),
            P(DP),
            P(),
            everywhere,
            everywhere,
            P(),
            everywhere,
            everywhere,
            everywhere,
            P(),
            P(),
            P(),
        ),
        out_specs=(P(DP, TM, None), P(DP, None), everywhere, P(DP)),
        check_vma=False,
    )
```

```python
import functools

import jax
import jax.numpy as jnp
import numpy as np
from jax import lax
from jax.experimental import pallas as pl
from jax.experimental.pallas import tpu as pltpu
from jax.sharding import Mesh
from jax.sharding import PartitionSpec as P

VHEADS = 16
THEADS = 16
HEAD = 88
LANES = 128
PIECE = 48
LOG2E = 1.4426950408889634

AXES = ("x", "h", "c", "y", "l")
DP = ("x", "h", "c")
TM = ("y", "l")
PLANE = ("h", "c", "y", "l")


def norm_rows(values, gain):
    full = values.astype(jnp.float32)
    scale = lax.rsqrt(jnp.mean(full * full, axis=-1, keepdims=True) + 1e-06)
    return (full * scale * gain).astype(jnp.bfloat16)


def swap(value, axis):
    return lax.ppermute(value, axis, [(0, 1), (1, 0)])


def dot(a, b):
    return jnp.dot(a, b, preferred_element_type=jnp.float32)


def dot_t(a, b):
    return lax.dot_general(a, b, (((1,), (1,)), ((), ())), preferred_element_type=jnp.float32)


def value_order():
    order = np.zeros((2 * LANES, 5 * LANES), np.float32)
    for head in range(2):
        for feature in range(HEAD):
            to = feature // 11 % 2 * PIECE + feature // 22 * 12 + feature % 11
            if feature < 80:
                source = LANES * (2 * head + feature // 40) + HEAD + feature % 40
            else:
                source = 4 * LANES + 8 * head + feature - 80
            order[LANES * head + to, source] = 1.0
    return jnp.asarray(order, jnp.bfloat16)


def video_qkv_kernel(places, order_hbm, *refs):
    blocks, own, other, qk_ref, vt_ref, x, w, last, order, sems = refs[:8], *refs[8:]
    wide = 2 * LANES
    depth = w.shape[0]
    core = places[8]
    copies = []
    for side, columns in ((core, own), (1 - core, other)):
        lanes = pl.ds(pl.multiple_of(wide * side, LANES), wide)
        copies.append((columns.at[pl.ds(0, depth)], w.at[:, lanes]))
        copies.append((columns.at[pl.ds(depth, LANES), pl.ds(0, LANES)], last.at[side]))
    copies.append((order_hbm, order))
    for j in range(8):
        copies.append((blocks[j], x.at[j]))
    copies = [pltpu.make_async_copy(a, b, sems.at[n]) for n, (a, b) in enumerate(copies)]
    for copy in copies:
        copy.start()
    group = lax.broadcasted_iota(jnp.int32, (depth, LANES), 0) // 11
    lane = lax.broadcasted_iota(jnp.int32, (depth, LANES), 1)
    row = lax.broadcasted_iota(jnp.int32, (depth, LANES), 0)
    chosen = jnp.where(group == lane, 1.0, 0.0).astype(jnp.bfloat16)
    mine = lane // 8 == row % 11
    source = lax.broadcasted_iota(jnp.int32, (LANES, LANES), 0)
    to = lax.broadcasted_iota(jnp.int32, (LANES, LANES), 1)
    for copy in copies[:4]:
        copy.wait()
    tail = jnp.zeros((depth, LANES), jnp.float32)
    for head in range(2):
        rows_of = jnp.where(mine, dot(chosen, last[head]), 0.0).astype(jnp.bfloat16)
        fold = jnp.where((source % 8 + 8 * head == to) & (source < HEAD), 1.0, 0.0).astype(jnp.bfloat16)
        tail = tail + dot(rows_of, fold)
    tail = tail.astype(jnp.bfloat16)
    for copy in copies[4:]:
        copy.wait()
    rows = x.shape[1]
    tokens = x[...].reshape(8 * rows, depth)
    whole = dot(tokens, w[...]).astype(jnp.bfloat16)
    apart = dot(tokens, tail).astype(jnp.bfloat16)
    is_query = lax.broadcasted_iota(jnp.int32, (rows, LANES), 1) < HEAD
    for j in range(8):
        some = whole[rows * j : rows * (j + 1)]
        at = places[j]
        values = dot_t(order[...], jnp.concatenate([some, apart[rows * j : rows * (j + 1)]], axis=1))
        for head in range(2):
            cols = wide * head
            q = some[:, cols : cols + LANES]
            qk_ref[at, :, cols : cols + LANES] = jnp.where(is_query, q, jnp.zeros_like(q))
            qk_ref[at, :, cols + LANES : cols + wide] = some[:, cols + LANES : cols + wide]
            vt_ref[at, head] = values[LANES * head : LANES * (head + 1)].astype(jnp.bfloat16)


def video_qkv(places, blocks, own, other):
    rows, width = blocks[0].shape
    vmem = pl.BlockSpec(memory_space=pltpu.VMEM)
    return pl.pallas_call(
        video_qkv_kernel,
        out_shape=(
            jax.ShapeDtypeStruct((8, rows, 4 * LANES), jnp.bfloat16),
            jax.ShapeDtypeStruct((8, 2, LANES, rows), jnp.bfloat16),
        ),
        in_specs=[pl.BlockSpec(memory_space=pltpu.SMEM)] + [pl.BlockSpec(memory_space=pl.ANY)] * 11,
        out_specs=(vmem, vmem),
        scratch_shapes=[
            pltpu.VMEM((8, rows, width), jnp.bfloat16),
            pltpu.VMEM((width, 4 * LANES), jnp.bfloat16),
            pltpu.VMEM((2, LANES, LANES), jnp.bfloat16),
            pltpu.VMEM((2 * LANES, 5 * LANES), jnp.bfloat16),
            pltpu.SemaphoreType.DMA((13,)),
        ],
        compiler_params=pltpu.CompilerParams(vmem_limit_bytes=60 * 2**20),
        cost_estimate=pl.CostEstimate(flops=5 * 10**9, bytes_accessed=10**7, transcendentals=0),
        name="video_qkv",
    )(places, value_order(), *blocks, own, other)


def video_attend_kernel(lists, qk_hbm, vt_hbm, out_ref, qk, vt, pairs, scores, tops, totals, accs, sems):
    copies = [pltpu.make_async_copy(qk_hbm, qk, sems.at[0]), pltpu.make_async_copy(vt_hbm, vt, sems.at[1])]
    for copy in copies:
        copy.start()
    rows = qk.shape[1]
    count = jnp.int32(0)
    for i in range(8):
        for k in range(8):
            pairs[0, count] = jnp.int32(i)
            pairs[1, count] = lists[i, k]
            pairs[2, count] = jnp.int32(k == 0)
            count = count + jnp.where(lists[i, k] >= 0, 1, 0)

    for copy in copies:
        copy.wait()
    factor = jnp.float32(LOG2E / HEAD**0.5)

    def score(i, j, head):
        at = 2 * LANES * head
        return dot_t(qk[j, :, at + LANES : at + 2 * LANES], qk[i, :, at : at + LANES])

    for head in range(2):
        scores[0, head] = score(pairs[0, 0], pairs[1, 0], head)

    def one_pair(e, carry):
        slot = lax.rem(e, 2)
        i, j, first = pairs[0, e], pairs[1, e], pairs[2, e] == 1
        later = jnp.minimum(e + 1, count - 1)
        next_i, next_j = pairs[0, later], pairs[1, later]
        for head in range(2):
            ahead = score(next_i, next_j, head)
            s = scores[slot, head]
            top = jnp.where(first, jnp.full((1, rows), -1e30, jnp.float32), tops[head])
            top_new = jnp.maximum(top, jnp.max(s, axis=0, keepdims=True))
            shift = top_new * factor
            weights = jnp.exp2(s * factor - shift)
            old = jnp.exp2(top * factor - shift)
            tops[head] = top_new
            totals[head] = jnp.where(first, 0.0, totals[head]) * old + jnp.sum(weights, axis=0, keepdims=True)
            accs[head] = jnp.where(first, 0.0, accs[head]) * old + dot(vt[j, head], weights.astype(jnp.bfloat16))
            scores[1 - slot, head] = ahead

        @pl.when((e == count - 1) | (next_i != i))
        def _():
            for head in range(2):
                mixed = (accs[head] / totals[head]).astype(jnp.bfloat16)
                for l in range(2):
                    to = 2 * PIECE * l + PIECE * head
                    out_ref[i, to : to + PIECE] = mixed[PIECE * l : PIECE * (l + 1)]

        return carry

    lax.fori_loop(0, count, one_pair, 0)


def video_attend(lists, qk, vt):
    rows = qk.shape[1]
    vmem = pl.BlockSpec(memory_space=pltpu.VMEM)
    return pl.pallas_call(
        video_attend_kernel,
        out_shape=jax.ShapeDtypeStruct((8, 4 * PIECE, rows), jnp.bfloat16),
        in_specs=[pl.BlockSpec(memory_space=pltpu.SMEM)] + [pl.BlockSpec(memory_space=pl.ANY)] * 2,
        out_specs=vmem,
        scratch_shapes=[
            pltpu.VMEM(qk.shape, jnp.bfloat16),
            pltpu.VMEM(vt.shape, jnp.bfloat16),
            pltpu.SMEM((3, 72), jnp.int32),
            pltpu.VMEM((2, 2, rows, rows), jnp.float32),
            pltpu.VMEM((2, 1, rows), jnp.float32),
            pltpu.VMEM((2, 1, rows), jnp.float32),
            pltpu.VMEM((2, LANES, rows), jnp.float32),
            pltpu.SemaphoreType.DMA((2,)),
        ],
        compiler_params=pltpu.CompilerParams(vmem_limit_bytes=60 * 2**20),
        cost_estimate=pl.CostEstimate(flops=4 * 10**9, bytes_accessed=4 * 10**6, transcendentals=5 * 10**6),
        name="video_attend",
    )(lists, qk, vt)


def video_out_kernel(places, power, mixed_hbm, tokens_hbm, own, other, out_ref, sums_ref, w, mixed, tokens, sems):
    c = places[4]
    copies = [(mixed_hbm, mixed), (tokens_hbm, tokens)]
    for n in range(4):
        copies.append((own.at[:, n], w.at[c, :, places[n]]))
        copies.append((other.at[:, n], w.at[1 - c, :, places[n]]))
    copies = [pltpu.make_async_copy(a, b, sems.at[n]) for n, (a, b) in enumerate(copies)]
    for copy in copies:
        copy.start()
    for copy in copies:
        copy.wait()
    p = power[0]
    for half, (low, high, skip) in enumerate(((0, 768, 0), (768, 1408, 128))):
        acc = tokens[:, low:high].astype(jnp.float32)
        total = jnp.zeros_like(acc)
        for t in range(8):
            total = total + lax.dot_general(
                mixed[t],
                w[half, t // 2, t % 2 * 2 : t % 2 * 2 + 2].reshape(4 * PIECE, 768)[:, skip:],
                (((0,), (0,)), ((), ())),
                preferred_element_type=jnp.float32,
            )
        out = (acc + total).astype(jnp.bfloat16)
        out_ref[:, low:high] = out
        grown = jnp.exp2(jnp.log2(jnp.maximum(out.astype(jnp.float32), 1e-06)) * p)
        sums_ref[:, low:high] = jnp.broadcast_to(jnp.sum(grown, axis=0, keepdims=True), (8, high - low))


def video_project(places, power, mixed, tokens, own, other):
    rows, width = tokens.shape
    vmem = pl.BlockSpec(memory_space=pltpu.VMEM)
    smem = pl.BlockSpec(memory_space=pltpu.SMEM)
    hbm = pl.BlockSpec(memory_space=pl.ANY)
    return pl.pallas_call(
        video_out_kernel,
        out_shape=(
            jax.ShapeDtypeStruct((rows, width), jnp.bfloat16),
            jax.ShapeDtypeStruct((8, width), jnp.float32),
        ),
        in_specs=[smem, smem, hbm, hbm, hbm, hbm],
        out_specs=(vmem, vmem),
        scratch_shapes=[
            pltpu.VMEM((2, 4, 4, 2 * PIECE, 768), jnp.bfloat16),
            pltpu.VMEM(mixed.shape, jnp.bfloat16),
            pltpu.VMEM(tokens.shape, jnp.bfloat16),
            pltpu.SemaphoreType.DMA((10,)),
        ],
        compiler_params=pltpu.CompilerParams(vmem_limit_bytes=60 * 2**20),
        cost_estimate=pl.CostEstimate(flops=10**9, bytes_accessed=10**7, transcendentals=10**6),
        name="video_out",
    )(places, power, mixed, tokens, own, other)


def in_weight_order(rows):
    source = lax.broadcasted_iota(jnp.int32, (LANES, LANES), 0)
    to = lax.broadcasted_iota(jnp.int32, (LANES, LANES), 1)
    wanted = (source // 8) % 2 * 64 + source // 16 * 8 + source % 8
    order = jnp.where(to == wanted, 1.0, 0.0).astype(jnp.bfloat16)
    parts = [dot(rows[:, at : at + LANES], order).astype(jnp.bfloat16) for at in range(0, rows.shape[1], LANES)]
    return jnp.concatenate(parts, axis=1)


def text_kernel(core, tokens_ref, gain_ref, own, other, embed_ref, w, mixed, sems):
    c = core[0]
    sides = (c, 1 - c)
    copies = [pltpu.make_async_copy(part, w.at[side], sems.at[n]) for n, (part, side) in enumerate(zip((own, other), sides))]
    for copy in copies:
        copy.start()
    rows, width = tokens_ref.shape
    half = width // 2
    length = 64
    tile = 256
    tokens = tokens_ref[...].astype(jnp.float32)
    scale = lax.rsqrt(jnp.mean(tokens * tokens, axis=-1, keepdims=True) + 1e-06)
    normed = in_weight_order((tokens * scale * gain_ref[...]).astype(jnp.bfloat16))
    same = (lax.broadcasted_iota(jnp.int32, (2 * tile, tile), 0) % tile // length) == (
        lax.broadcasted_iota(jnp.int32, (2 * tile, tile), 1) // length
    )
    low = lax.broadcasted_iota(jnp.int32, (tile, LANES), 1) < length
    factor = jnp.float32(LOG2E / 8.0)
    for copy, side in zip(copies, sides):
        copy.wait()
        qkv = dot(normed, w[side, :, : 3 * half]).astype(jnp.bfloat16)
        for pair in range(half // LANES):
            at = pair * LANES
            to = pl.ds(pl.multiple_of(side * half + at, LANES), LANES)
            for sub in range(0, rows, tile):
                q = qkv[sub : sub + tile, at : at + LANES]
                key = qkv[sub : sub + tile, half + at : half + at + LANES]
                value = qkv[sub : sub + tile, 2 * half + at : 2 * half + at + LANES]
                none = jnp.zeros_like(q)
                s = dot_t(jnp.concatenate([jnp.where(low, q, none), jnp.where(low, none, q)], axis=0), key)
                s = jnp.where(same, s, jnp.float32(-1e30))
                top = jnp.max(s, axis=1, keepdims=True)
                weights = jnp.exp2((s - top) * factor)
                total = jnp.sum(weights, axis=1, keepdims=True)
                o = dot(weights.astype(jnp.bfloat16), value) / total
                mixed[sub : sub + tile, to] = jnp.where(low, o[:tile], o[tile:]).astype(jnp.bfloat16)
    whole = in_weight_order(mixed[...])
    means = []
    square = jnp.zeros((rows // length, 1), jnp.float32)
    for side in range(2):
        cols = slice(side * half, (side + 1) * half)
        projected = dot(whole, w[side, :, 3 * half :])
        out = (tokens_ref[:, cols].astype(jnp.float32) + projected).astype(jnp.bfloat16).astype(jnp.float32)
        mean = jnp.sum(out.reshape(rows // length, length, half), axis=1) * (1.0 / length)
        square = square + jnp.sum(mean * mean, axis=1, keepdims=True)
        means.append(mean)
    inverse = lax.rsqrt(square + 1e-06)
    for side in range(2):
        embed_ref[:, side * half : (side + 1) * half] = means[side] * inverse


def text_layer(core, tokens, gain, own, other):
    rows, width = tokens.shape
    vmem = pl.BlockSpec(memory_space=pltpu.VMEM)
    hbm = pl.BlockSpec(memory_space=pl.ANY)
    return pl.pallas_call(
        text_kernel,
        out_shape=jax.ShapeDtypeStruct((rows // 64, width), jnp.float32),
        in_specs=[pl.BlockSpec(memory_space=pltpu.SMEM), vmem, vmem, hbm, hbm],
        out_specs=vmem,
        scratch_shapes=[
            pltpu.VMEM((2,) + own.shape, jnp.bfloat16),
            pltpu.VMEM((rows, width), jnp.bfloat16),
            pltpu.SemaphoreType.DMA((2,)),
        ],
        compiler_params=pltpu.CompilerParams(vmem_limit_bytes=50 * 2**20),
        cost_estimate=pl.CostEstimate(flops=17 * 10**9, bytes_accessed=10**7, transcendentals=4 * 10**6),
        name="text_layer",
    )(core, tokens, gain, own, other)


def logits_kernel(floats, sums, texts, columns, out_ref, *, tokens):
    total = sums[0:1]
    pooled = jnp.exp(jnp.log(total * (1.0 / tokens)) * floats[0]).astype(jnp.bfloat16)
    proj = dot(jnp.broadcast_to(pooled, (16, pooled.shape[1])), columns[...])[:8]
    count = texts.shape[0]
    out_ref[:, 0, :count] = lax.dot_general(
        proj,
        texts[...].astype(jnp.float32),
        (((1,), (1,)), ((), ())),
        precision=lax.Precision.HIGHEST,
        preferred_element_type=jnp.float32,
    )
    out_ref[:, 0, count:] = proj


def partial_logits(floats, sums, texts, columns, tokens):
    smem = pl.BlockSpec(memory_space=pltpu.SMEM)
    vmem = pl.BlockSpec(memory_space=pltpu.VMEM)
    return pl.pallas_call(
        functools.partial(logits_kernel, tokens=tokens),
        out_shape=jax.ShapeDtypeStruct((8, 1, texts.shape[0] + LANES), jnp.float32),
        in_specs=[smem, vmem, vmem, vmem],
        out_specs=vmem,
        compiler_params=pltpu.CompilerParams(vmem_limit_bytes=32 * 2**20),
        cost_estimate=pl.CostEstimate(flops=10**7, bytes_accessed=10**6, transcendentals=10**4),
        name="partial_logits",
    )(floats, sums, texts, columns)


def loss_kernel(positive, floats, parts, embed_ref, loss_ref):
    count = parts.shape[2] - LANES
    proj = parts[:, 0, count:]
    inverse = lax.rsqrt(jnp.sum(proj * proj, keepdims=True) + 1e-06)
    for t in range(8):
        embed_ref[:, LANES * t : LANES * (t + 1)] = proj[t : t + 1] * inverse
    raw = jnp.sum(parts[:, 0, :count], axis=0, keepdims=True)
    logits = raw * (inverse * jnp.exp(jnp.full((1, 1), floats[1]))) + floats[2]
    ids = lax.broadcasted_iota(jnp.int32, (1, count), 1)
    z = jnp.where(ids == positive[0], -logits, logits)
    terms = jnp.maximum(z, 0.0) + jnp.log1p(jnp.exp(-jnp.abs(z)))
    loss_ref[...] = jnp.sum(terms, axis=1, keepdims=True) * (1.0 / 128.0)


def embed_and_loss(positive, floats, parts):
    smem = pl.BlockSpec(memory_space=pltpu.SMEM)
    vmem = pl.BlockSpec(memory_space=pltpu.VMEM)
    return pl.pallas_call(
        loss_kernel,
        out_shape=(
            jax.ShapeDtypeStruct((1, 8 * LANES), jnp.float32),
            jax.ShapeDtypeStruct((1, 1), jnp.float32),
        ),
        in_specs=[smem, smem, vmem],
        out_specs=(vmem, vmem),
        cost_estimate=pl.CostEstimate(flops=10**6, bytes_accessed=10**5, transcendentals=10**4),
        name="embed_and_loss",
    )(positive, floats, parts)


def pack_kernel(listed, w_heads, w_out, w_embed, w_text, w_text_out, shared_ref, columns_ref, embed_ref, held):
    rows = w_heads.shape[0]
    half = w_text_out.shape[1] // 2
    width = w_heads.shape[1] // 3
    lane = lax.broadcasted_iota(jnp.int32, (rows, LANES), 1)
    row = lax.broadcasted_iota(jnp.int32, (rows, LANES), 0)
    spread = jnp.where(
        lax.broadcasted_iota(jnp.int32, (8, LANES), 1) % 8 == lax.broadcasted_iota(jnp.int32, (8, LANES), 0), 1.0, 0.0
    ).astype(jnp.bfloat16)
    shared_ref[...] = jnp.zeros_like(shared_ref)
    embed_ref[...] = jnp.zeros_like(embed_ref)
    for c in range(2):
        piece = lambda i: w_text[:, 2 * half * i + half * c : 2 * half * i + half * (c + 1)].astype(jnp.float32)
        upper = jnp.concatenate([piece(0), piece(1)], axis=1)
        lower = jnp.concatenate([piece(2), w_text_out[:, half * c : half * (c + 1)].astype(jnp.float32)], axis=1)
        text = jnp.concatenate([upper, lower], axis=0).astype(jnp.bfloat16)
        for y in range(4):
            shared_ref[4 * c + y, :, :1024] = text
            shared_ref[4 * c + y, :rows, 1024:] = w_out[:, 640 * c : 640 * c + 768]
        for t in range(8):
            at = HEAD * (2 * t + c)
            q, k, v = (w_heads[:, width * i + at : width * i + at + HEAD] for i in range(3))
            held[0:rows] = jnp.concatenate([q.astype(jnp.float32), v[:, :40].astype(jnp.float32)], axis=1)
            held[rows : 2 * rows] = jnp.concatenate([k.astype(jnp.float32), v[:, 40:80].astype(jnp.float32)], axis=1)
            rest = jnp.where(lane // 8 == row, dot(v[:, 80:], spread), 0.0)
            held[2 * rows : 2 * rows + 1] = jnp.sum(rest, axis=0, keepdims=True)
            held[2 * rows + 1 :] = listed[...]
            value = held[...].astype(jnp.bfloat16)
            for plane in range(8):
                columns_ref[16 * plane + 8 * c + t] = value
                embed_ref[16 * plane + 8 * c + t, :rows] = w_embed[:, LANES * t : LANES * (t + 1)]


def pack_weights(listed, w_heads, *weights):
    vmem = pl.BlockSpec(memory_space=pltpu.VMEM)
    rows = w_heads.shape[0]
    return pl.pallas_call(
        pack_kernel,
        out_shape=(
            jax.ShapeDtypeStruct((8, 16, 1792), jnp.bfloat16),
            jax.ShapeDtypeStruct((128, 2 * rows + 2, LANES), jnp.bfloat16),
            jax.ShapeDtypeStruct((128, 16, LANES), jnp.bfloat16),
        ),
        in_specs=[vmem] * 6,
        out_specs=(vmem,) * 3,
        scratch_shapes=[pltpu.VMEM((2 * rows + 2, LANES), jnp.float32)],
        compiler_params=pltpu.CompilerParams(vmem_limit_bytes=32 * 2**20),
        cost_estimate=pl.CostEstimate(flops=10**6, bytes_accessed=3 * 10**6, transcendentals=0),
        name="pack_weights",
    )(listed, w_heads, *weights)


def per_device(
    video_tokens,
    text_tokens,
    block_lists,
    positive_text,
    video_gain,
    w_video_qkv,
    w_video_out,
    text_gain,
    w_text_qkv,
    w_text_out,
    w_embed,
    gem_power,
    log_scale,
    logit_bias,
):
    h, c = lax.axis_index("h"), lax.axis_index("c")
    x, y, l = lax.axis_index("x"), lax.axis_index("y"), lax.axis_index("l")
    t = 2 * y + l
    flat = video_tokens[0]

    normed = norm_rows(flat, video_gain)
    up = [(i, (i + 1) % 4) for i in range(4)]
    down = [(i, (i - 1) % 4) for i in range(4)]
    own_m = lax.ppermute(normed, "y", up)
    own_p = lax.ppermute(normed, "y", down)
    par = swap(normed, "l")

    listed = jnp.pad(block_lists[0].astype(jnp.float32), ((0, 0), (0, LANES - 8)))
    shared, columns, embed = pack_weights(listed, w_video_qkv, w_video_out, w_embed, w_text_qkv, w_text_out)
    shared = lax.all_to_all(shared, ("c", "y"), 0, 0)
    shared, columns, own_m, own_p, par = lax.optimization_barrier((shared, columns, own_m, own_p, par))
    own_o = lax.ppermute(own_m, "y", up)
    par_m = swap(own_m, "l")
    par_p = lax.ppermute(par, "y", down)
    w_out = shared[:, :12, 1024:].reshape(2 * PIECE, 768)
    out_l = swap(w_out, "l")
    par_p, out_l = lax.optimization_barrier((par_p, out_l))
    par_o = lax.ppermute(par_p, "y", down)

    text = jnp.transpose(shared[:, :, :1024].reshape(8, 2, 8, 1024), (0, 2, 1, 3)).reshape(64, 2048)
    text = lax.all_gather(text, ("x", "h", "l"), axis=0, tiled=True)

    columns = lax.all_to_all(columns, AXES, 0, 0)
    columns, own_o, par_m, par_p, par_o, out_l = lax.optimization_barrier(
        (columns, own_o, par_m, par_p, par_o, out_l)
    )
    w_out = jnp.stack([w_out, out_l])
    out_h = swap(w_out, "h")
    count = w_video_qkv.shape[0]
    lists = columns[:, 2 * count + 1, :8].reshape(16, 8, 8)
    lists = lax.dynamic_index_in_dim(lists, 4 * x + 2 * h + c, 0, keepdims=False).astype(jnp.int32)
    last = jnp.pad(columns[:, 2 * count], ((0, 0), (0, LANES)))
    columns = jnp.concatenate([columns[:, :count], columns[:, count : 2 * count]], axis=2).reshape(-1, 2 * LANES)
    columns = jnp.concatenate([columns, last])
    columns_other = swap(columns, "c")

    arrived = [normed, own_m, own_p, par, par_m, par_p, own_o, par_o]
    turn = lambda dy, other: 2 * ((y + dy) % 4) + (1 - l if other else l)
    turns = [turn(0, 0), turn(3, 0), turn(1, 0), turn(0, 1), turn(3, 1), turn(1, 1), turn(2, 0), turn(2, 1)]
    places = jnp.stack(turns + [c]).astype(jnp.int32)
    qk, vt = video_qkv(places, arrived, columns, columns_other)
    text, qk, vt, out_h = lax.optimization_barrier((text, qk, vt, out_h))
    text_other = swap(text, "c")
    w_out = lax.all_gather(jnp.concatenate([w_out, out_h]), "x", axis=0)
    out_places = jnp.stack([2 * h + l, 2 * h + 1 - l, 2 - 2 * h + l, 3 - 2 * h - l, c]).astype(jnp.int32)
    mixed = video_attend(lists, qk, vt)

    core = c.astype(jnp.int32)[None]
    mixed, tokens = lax.optimization_barrier((mixed, text_tokens))
    mixed = lax.all_to_all(mixed, TM, 0, 0)

    texts, length, twidth = text_tokens.shape
    text_embed = text_layer(
        core, tokens.reshape(texts * length, twidth), text_gain[None], text, text_other
    )
    mixed, text_embed, w_out = lax.optimization_barrier((mixed, text_embed, w_out))
    out_other = swap(w_out, "c")
    sent = jnp.transpose(text_embed.astype(jnp.bfloat16).reshape(texts, 8, LANES), (1, 0, 2))
    sent = jnp.broadcast_to(sent[None], (16,) + sent.shape).reshape(128, texts, LANES)
    sent = lax.all_to_all(jnp.concatenate([sent, embed], axis=1), AXES, 0, 0)
    all_texts = sent[:, :texts].reshape(128 * texts, LANES)
    embed = sent[:, texts : texts + w_embed.shape[0]].reshape(-1, LANES)

    video_out, sums = video_project(out_places, gem_power, mixed, flat, w_out, out_other)
    sums = sums + swap(sums, "l")
    sums = sums + sum(lax.ppermute(sums, "y", [(i, (i + k) % 4) for i in range(4)]) for k in (1, 2, 3))
    floats = jnp.stack([1.0 / gem_power[0], log_scale[0], logit_bias[0]])
    parts = partial_logits(floats, sums, all_texts, embed, 8 * flat.shape[0])
    parts = lax.all_to_all(parts, TM, 0, 0).reshape(parts.shape)
    video_embed, clip_loss = embed_and_loss(positive_text, floats, parts)
    return (video_out[None], video_embed, text_embed, clip_loss[0])


def solution(mesh):
    fine = Mesh(mesh.devices.reshape(4, 2, 2, 4, 2), AXES)
    everywhere = P(DP + TM, None)
    return jax.shard_map(
        per_device,
        mesh=fine,
        in_specs=(
            P(DP, TM, None),
            P(DP + TM, None, None),
            P(DP, TM, None),
            P(DP),
            P(),
            everywhere,
            everywhere,
            P(),
            everywhere,
            everywhere,
            everywhere,
            P(),
            P(),
            P(),
        ),
        out_specs=(P(DP, TM, None), P(DP, None), everywhere, P(DP)),
        check_vma=False,
    )
```

```python
import functools

import jax
import jax.numpy as jnp
import numpy as np
from jax import lax
from jax.experimental import pallas as pl
from jax.experimental.pallas import tpu as pltpu
from jax.sharding import Mesh
from jax.sharding import PartitionSpec as P

VHEADS = 16
THEADS = 16
HEAD = 88
LANES = 128
PIECE = 48
LOG2E = 1.4426950408889634

AXES = ("x", "h", "c", "y", "l")
DP = ("x", "h", "c")
TM = ("y", "l")
PLANE = ("h", "c", "y", "l")


def norm_rows(values, gain):
    full = values.astype(jnp.float32)
    scale = lax.rsqrt(jnp.mean(full * full, axis=-1, keepdims=True) + 1e-06)
    return (full * scale * gain).astype(jnp.bfloat16)


def swap(value, axis):
    return lax.ppermute(value, axis, [(0, 1), (1, 0)])


def dot(a, b):
    return jnp.dot(a, b, preferred_element_type=jnp.float32)


def dot_t(a, b):
    return lax.dot_general(a, b, (((1,), (1,)), ((), ())), preferred_element_type=jnp.float32)


def value_order():
    order = np.zeros((2 * LANES, 5 * LANES), np.float32)
    for head in range(2):
        for feature in range(HEAD):
            to = feature // 11 % 2 * PIECE + feature // 22 * 12 + feature % 11
            if feature < 80:
                source = LANES * (2 * head + feature // 40) + HEAD + feature % 40
            else:
                source = 4 * LANES + 8 * head + feature - 80
            order[LANES * head + to, source] = 1.0
    return jnp.asarray(order, jnp.bfloat16)


def video_qkv_kernel(places, order_hbm, *refs):
    blocks, own, other, qk_ref, vt_ref, x, w, last, order, sems = refs[:8], *refs[8:]
    wide = 2 * LANES
    depth = w.shape[0]
    core = places[8]
    copies = []
    for side, columns in ((core, own), (1 - core, other)):
        lanes = pl.ds(pl.multiple_of(wide * side, LANES), wide)
        copies.append((columns.at[pl.ds(0, depth)], w.at[:, lanes]))
        copies.append((columns.at[pl.ds(depth, LANES), pl.ds(0, LANES)], last.at[side]))
    copies.append((order_hbm, order))
    for j in range(8):
        copies.append((blocks[j], x.at[j]))
    copies = [pltpu.make_async_copy(a, b, sems.at[n]) for n, (a, b) in enumerate(copies)]
    for copy in copies:
        copy.start()
    group = lax.broadcasted_iota(jnp.int32, (depth, LANES), 0) // 11
    lane = lax.broadcasted_iota(jnp.int32, (depth, LANES), 1)
    row = lax.broadcasted_iota(jnp.int32, (depth, LANES), 0)
    chosen = jnp.where(group == lane, 1.0, 0.0).astype(jnp.bfloat16)
    mine = lane // 8 == row % 11
    source = lax.broadcasted_iota(jnp.int32, (LANES, LANES), 0)
    to = lax.broadcasted_iota(jnp.int32, (LANES, LANES), 1)
    for copy in copies[:4]:
        copy.wait()
    tail = jnp.zeros((depth, LANES), jnp.float32)
    for head in range(2):
        rows_of = jnp.where(mine, dot(chosen, last[head]), 0.0).astype(jnp.bfloat16)
        fold = jnp.where((source % 8 + 8 * head == to) & (source < HEAD), 1.0, 0.0).astype(jnp.bfloat16)
        tail = tail + dot(rows_of, fold)
    tail = tail.astype(jnp.bfloat16)
    for copy in copies[4:]:
        copy.wait()
    rows = x.shape[1]
    tokens = x[...].reshape(8 * rows, depth)
    whole = dot(tokens, w[...]).astype(jnp.bfloat16)
    apart = dot(tokens, tail).astype(jnp.bfloat16)
    is_query = lax.broadcasted_iota(jnp.int32, (rows, LANES), 1) < HEAD
    for j in range(8):
        some = whole[rows * j : rows * (j + 1)]
        at = places[j]
        values = dot_t(order[...], jnp.concatenate([some, apart[rows * j : rows * (j + 1)]], axis=1))
        for head in range(2):
            cols = wide * head
            q = some[:, cols : cols + LANES]
            qk_ref[at, :, cols : cols + LANES] = jnp.where(is_query, q, jnp.zeros_like(q))
            qk_ref[at, :, cols + LANES : cols + wide] = some[:, cols + LANES : cols + wide]
            vt_ref[at, head] = values[LANES * head : LANES * (head + 1)].astype(jnp.bfloat16)


def video_qkv(places, blocks, own, other):
    rows, width = blocks[0].shape
    vmem = pl.BlockSpec(memory_space=pltpu.VMEM)
    return pl.pallas_call(
        video_qkv_kernel,
        out_shape=(
            jax.ShapeDtypeStruct((8, rows, 4 * LANES), jnp.bfloat16),
            jax.ShapeDtypeStruct((8, 2, LANES, rows), jnp.bfloat16),
        ),
        in_specs=[pl.BlockSpec(memory_space=pltpu.SMEM)] + [pl.BlockSpec(memory_space=pl.ANY)] * 11,
        out_specs=(vmem, vmem),
        scratch_shapes=[
            pltpu.VMEM((8, rows, width), jnp.bfloat16),
            pltpu.VMEM((width, 4 * LANES), jnp.bfloat16),
            pltpu.VMEM((2, LANES, LANES), jnp.bfloat16),
            pltpu.VMEM((2 * LANES, 5 * LANES), jnp.bfloat16),
            pltpu.SemaphoreType.DMA((13,)),
        ],
        compiler_params=pltpu.CompilerParams(vmem_limit_bytes=60 * 2**20),
        cost_estimate=pl.CostEstimate(flops=5 * 10**9, bytes_accessed=10**7, transcendentals=0),
        name="video_qkv",
    )(places, value_order(), *blocks, own, other)


def video_attend_kernel(lists, qk_hbm, vt_hbm, out_ref, qk, vt, pairs, scores, tops, totals, accs, sems):
    copies = [pltpu.make_async_copy(qk_hbm, qk, sems.at[0]), pltpu.make_async_copy(vt_hbm, vt, sems.at[1])]
    for copy in copies:
        copy.start()
    rows = qk.shape[1]
    count = jnp.int32(0)
    for i in range(8):
        for k in range(8):
            pairs[0, count] = jnp.int32(i)
            pairs[1, count] = lists[i, k]
            pairs[2, count] = jnp.int32(k == 0)
            count = count + jnp.where(lists[i, k] >= 0, 1, 0)

    for copy in copies:
        copy.wait()
    factor = jnp.float32(LOG2E / HEAD**0.5)

    def score(i, j, head):
        at = 2 * LANES * head
        return dot_t(qk[j, :, at + LANES : at + 2 * LANES], qk[i, :, at : at + LANES])

    for head in range(2):
        scores[0, head] = score(pairs[0, 0], pairs[1, 0], head)

    def one_pair(e, carry):
        slot = lax.rem(e, 2)
        i, j, first = pairs[0, e], pairs[1, e], pairs[2, e] == 1
        later = jnp.minimum(e + 1, count - 1)
        next_i, next_j = pairs[0, later], pairs[1, later]
        for head in range(2):
            ahead = score(next_i, next_j, head)
            s = scores[slot, head]
            top = jnp.where(first, jnp.full((1, rows), -1e30, jnp.float32), tops[head])
            top_new = jnp.maximum(top, jnp.max(s, axis=0, keepdims=True))
            shift = top_new * factor
            weights = jnp.exp2(s * factor - shift)
            old = jnp.exp2(top * factor - shift)
            tops[head] = top_new
            totals[head] = jnp.where(first, 0.0, totals[head]) * old + jnp.sum(weights, axis=0, keepdims=True)
            accs[head] = jnp.where(first, 0.0, accs[head]) * old + dot(vt[j, head], weights.astype(jnp.bfloat16))
            scores[1 - slot, head] = ahead

        @pl.when((e == count - 1) | (next_i != i))
        def _():
            for head in range(2):
                mixed = (accs[head] / totals[head]).astype(jnp.bfloat16)
                for l in range(2):
                    to = 2 * PIECE * l + PIECE * head
                    out_ref[i, to : to + PIECE] = mixed[PIECE * l : PIECE * (l + 1)]

        return carry

    lax.fori_loop(0, count, one_pair, 0)


def video_attend(lists, qk, vt):
    rows = qk.shape[1]
    vmem = pl.BlockSpec(memory_space=pltpu.VMEM)
    return pl.pallas_call(
        video_attend_kernel,
        out_shape=jax.ShapeDtypeStruct((8, 4 * PIECE, rows), jnp.bfloat16),
        in_specs=[pl.BlockSpec(memory_space=pltpu.SMEM)] + [pl.BlockSpec(memory_space=pl.ANY)] * 2,
        out_specs=vmem,
        scratch_shapes=[
            pltpu.VMEM(qk.shape, jnp.bfloat16),
            pltpu.VMEM(vt.shape, jnp.bfloat16),
            pltpu.SMEM((3, 72), jnp.int32),
            pltpu.VMEM((2, 2, rows, rows), jnp.float32),
            pltpu.VMEM((2, 1, rows), jnp.float32),
            pltpu.VMEM((2, 1, rows), jnp.float32),
            pltpu.VMEM((2, LANES, rows), jnp.float32),
            pltpu.SemaphoreType.DMA((2,)),
        ],
        compiler_params=pltpu.CompilerParams(vmem_limit_bytes=60 * 2**20),
        cost_estimate=pl.CostEstimate(flops=4 * 10**9, bytes_accessed=4 * 10**6, transcendentals=5 * 10**6),
        name="video_attend",
    )(lists, qk, vt)


def video_out_kernel(places, power, mixed_hbm, tokens_hbm, own, other, out_ref, sums_ref, w, mixed, tokens, sems):
    c = places[8]
    copies = [(mixed_hbm, mixed), (tokens_hbm, tokens)]
    for n in range(4):
        copies.append((own.at[:, n], w.at[c, :, places[9 + n]]))
        copies.append((other.at[:, n], w.at[1 - c, :, places[9 + n]]))
    copies = [pltpu.make_async_copy(a, b, sems.at[n]) for n, (a, b) in enumerate(copies)]
    for copy in copies:
        copy.start()
    for copy in copies:
        copy.wait()
    p = power[0]
    for half, (low, high, skip) in enumerate(((0, 768, 0), (768, 1408, 128))):
        acc = tokens[:, low:high].astype(jnp.float32)
        total = lax.dot_general(
            mixed[...].reshape(32 * PIECE, mixed.shape[2]),
            w[half].reshape(32 * PIECE, 768)[:, skip:],
            (((0,), (0,)), ((), ())),
            preferred_element_type=jnp.float32,
        )
        out = (acc + total).astype(jnp.bfloat16)
        out_ref[:, low:high] = out
        grown = jnp.exp2(jnp.log2(jnp.maximum(out.astype(jnp.float32), 1e-06)) * p)
        sums_ref[:, low:high] = jnp.broadcast_to(jnp.sum(grown, axis=0, keepdims=True), (8, high - low))


def video_project(places, power, mixed, tokens, own, other):
    rows, width = tokens.shape
    vmem = pl.BlockSpec(memory_space=pltpu.VMEM)
    smem = pl.BlockSpec(memory_space=pltpu.SMEM)
    hbm = pl.BlockSpec(memory_space=pl.ANY)
    return pl.pallas_call(
        video_out_kernel,
        out_shape=(
            jax.ShapeDtypeStruct((rows, width), jnp.bfloat16),
            jax.ShapeDtypeStruct((8, width), jnp.float32),
        ),
        in_specs=[smem, smem, hbm, hbm, hbm, hbm],
        out_specs=(vmem, vmem),
        scratch_shapes=[
            pltpu.VMEM((2, 4, 4, 2 * PIECE, 768), jnp.bfloat16),
            pltpu.VMEM(mixed.shape, jnp.bfloat16),
            pltpu.VMEM(tokens.shape, jnp.bfloat16),
            pltpu.SemaphoreType.DMA((10,)),
        ],
        compiler_params=pltpu.CompilerParams(vmem_limit_bytes=60 * 2**20),
        cost_estimate=pl.CostEstimate(flops=10**9, bytes_accessed=10**7, transcendentals=10**6),
        name="video_out",
    )(places, power, mixed, tokens, own, other)


def in_weight_order(rows):
    source = lax.broadcasted_iota(jnp.int32, (LANES, LANES), 0)
    to = lax.broadcasted_iota(jnp.int32, (LANES, LANES), 1)
    wanted = (source // 8) % 2 * 64 + source // 16 * 8 + source % 8
    order = jnp.where(to == wanted, 1.0, 0.0).astype(jnp.bfloat16)
    parts = [dot(rows[:, at : at + LANES], order).astype(jnp.bfloat16) for at in range(0, rows.shape[1], LANES)]
    return jnp.concatenate(parts, axis=1)


def text_kernel(core, tokens_ref, gain_ref, own, other, embed_ref, w, mixed, sems):
    c = core[0]
    sides = (c, 1 - c)
    copies = [pltpu.make_async_copy(part, w.at[side], sems.at[n]) for n, (part, side) in enumerate(zip((own, other), sides))]
    for copy in copies:
        copy.start()
    rows, width = tokens_ref.shape
    half = width // 2
    length = 64
    tile = 256
    tokens = tokens_ref[...].astype(jnp.float32)
    scale = lax.rsqrt(jnp.mean(tokens * tokens, axis=-1, keepdims=True) + 1e-06)
    normed = in_weight_order((tokens * scale * gain_ref[...]).astype(jnp.bfloat16))
    same = (lax.broadcasted_iota(jnp.int32, (2 * tile, tile), 0) % tile // length) == (
        lax.broadcasted_iota(jnp.int32, (2 * tile, tile), 1) // length
    )
    low = lax.broadcasted_iota(jnp.int32, (tile, LANES), 1) < length
    factor = jnp.float32(LOG2E / 8.0)
    for copy, side in zip(copies, sides):
        copy.wait()
        qkv = dot(normed, w[side, :, : 3 * half]).astype(jnp.bfloat16)
        for pair in range(half // LANES):
            at = pair * LANES
            to = pl.ds(pl.multiple_of(side * half + at, LANES), LANES)
            for sub in range(0, rows, tile):
                q = qkv[sub : sub + tile, at : at + LANES]
                key = qkv[sub : sub + tile, half + at : half + at + LANES]
                value = qkv[sub : sub + tile, 2 * half + at : 2 * half + at + LANES]
                none = jnp.zeros_like(q)
                s = dot_t(jnp.concatenate([jnp.where(low, q, none), jnp.where(low, none, q)], axis=0), key)
                s = jnp.where(same, s, jnp.float32(-1e30))
                top = jnp.max(s, axis=1, keepdims=True)
                weights = jnp.exp2((s - top) * factor)
                total = jnp.sum(weights, axis=1, keepdims=True)
                o = dot(weights.astype(jnp.bfloat16), value) / total
                mixed[sub : sub + tile, to] = jnp.where(low, o[:tile], o[tile:]).astype(jnp.bfloat16)
    whole = in_weight_order(mixed[...])
    means = []
    square = jnp.zeros((rows // length, 1), jnp.float32)
    for side in range(2):
        cols = slice(side * half, (side + 1) * half)
        projected = dot(whole, w[side, :, 3 * half :])
        out = (tokens_ref[:, cols].astype(jnp.float32) + projected).astype(jnp.bfloat16).astype(jnp.float32)
        mean = jnp.sum(out.reshape(rows // length, length, half), axis=1) * (1.0 / length)
        square = square + jnp.sum(mean * mean, axis=1, keepdims=True)
        means.append(mean)
    inverse = lax.rsqrt(square + 1e-06)
    for side in range(2):
        embed_ref[:, side * half : (side + 1) * half] = means[side] * inverse


def text_layer(core, tokens, gain, own, other):
    rows, width = tokens.shape
    vmem = pl.BlockSpec(memory_space=pltpu.VMEM)
    hbm = pl.BlockSpec(memory_space=pl.ANY)
    return pl.pallas_call(
        text_kernel,
        out_shape=jax.ShapeDtypeStruct((rows // 64, width), jnp.float32),
        in_specs=[pl.BlockSpec(memory_space=pltpu.SMEM), vmem, vmem, hbm, hbm],
        out_specs=vmem,
        scratch_shapes=[
            pltpu.VMEM((2,) + own.shape, jnp.bfloat16),
            pltpu.VMEM((rows, width), jnp.bfloat16),
            pltpu.SemaphoreType.DMA((2,)),
        ],
        compiler_params=pltpu.CompilerParams(vmem_limit_bytes=50 * 2**20),
        cost_estimate=pl.CostEstimate(flops=17 * 10**9, bytes_accessed=10**7, transcendentals=4 * 10**6),
        name="text_layer",
    )(core, tokens, gain, own, other)


def logits_kernel(floats, sums, texts, columns, out_ref, *, tokens):
    total = sums[0:1]
    pooled = jnp.exp(jnp.log(total * (1.0 / tokens)) * floats[0]).astype(jnp.bfloat16)
    proj = dot(jnp.broadcast_to(pooled, (16, pooled.shape[1])), columns[...])[:8]
    count = texts.shape[0]
    parts = []
    rest = proj
    for _ in range(3):
        parts.append(rest.astype(jnp.bfloat16).astype(jnp.float32))
        rest = rest - parts[-1]
    raw = dot_t(jnp.concatenate(parts + [jnp.zeros_like(proj)], axis=0).astype(jnp.bfloat16), texts[...])
    out_ref[:, 0, :count] = raw[:8] + (raw[8:16] + raw[16:24])
    out_ref[:, 0, count:] = proj


def partial_logits(floats, sums, texts, columns, tokens):
    smem = pl.BlockSpec(memory_space=pltpu.SMEM)
    vmem = pl.BlockSpec(memory_space=pltpu.VMEM)
    return pl.pallas_call(
        functools.partial(logits_kernel, tokens=tokens),
        out_shape=jax.ShapeDtypeStruct((8, 1, texts.shape[0] + LANES), jnp.float32),
        in_specs=[smem, vmem, vmem, vmem],
        out_specs=vmem,
        compiler_params=pltpu.CompilerParams(vmem_limit_bytes=32 * 2**20),
        cost_estimate=pl.CostEstimate(flops=10**7, bytes_accessed=10**6, transcendentals=10**4),
        name="partial_logits",
    )(floats, sums, texts, columns)


def loss_kernel(positive, floats, parts, embed_ref, loss_ref):
    count = parts.shape[2] - LANES
    proj = parts[:, 0, count:]
    inverse = lax.rsqrt(jnp.sum(proj * proj, keepdims=True) + 1e-06)
    for t in range(8):
        embed_ref[:, LANES * t : LANES * (t + 1)] = proj[t : t + 1] * inverse
    raw = jnp.sum(parts[:, 0, :count], axis=0, keepdims=True)
    logits = raw * (inverse * jnp.exp(jnp.full((1, 1), floats[1]))) + floats[2]
    ids = lax.broadcasted_iota(jnp.int32, (1, count), 1)
    z = jnp.where(ids == positive[0], -logits, logits)
    terms = jnp.maximum(z, 0.0) + jnp.log1p(jnp.exp(-jnp.abs(z)))
    loss_ref[...] = jnp.sum(terms, axis=1, keepdims=True) * (1.0 / 128.0)


def embed_and_loss(positive, floats, parts):
    smem = pl.BlockSpec(memory_space=pltpu.SMEM)
    vmem = pl.BlockSpec(memory_space=pltpu.VMEM)
    return pl.pallas_call(
        loss_kernel,
        out_shape=(
            jax.ShapeDtypeStruct((1, 8 * LANES), jnp.float32),
            jax.ShapeDtypeStruct((1, 1), jnp.float32),
        ),
        in_specs=[smem, smem, vmem],
        out_specs=(vmem, vmem),
        cost_estimate=pl.CostEstimate(flops=10**6, bytes_accessed=10**5, transcendentals=10**4),
        name="embed_and_loss",
    )(positive, floats, parts)


def pack_kernel(listed, w_heads, w_out, w_embed, w_text, w_text_out, shared_ref, columns_ref, embed_ref, held):
    rows = w_heads.shape[0]
    half = w_text_out.shape[1] // 2
    width = w_heads.shape[1] // 3
    lane = lax.broadcasted_iota(jnp.int32, (rows, LANES), 1)
    row = lax.broadcasted_iota(jnp.int32, (rows, LANES), 0)
    spread = jnp.where(
        lax.broadcasted_iota(jnp.int32, (8, LANES), 1) % 8 == lax.broadcasted_iota(jnp.int32, (8, LANES), 0), 1.0, 0.0
    ).astype(jnp.bfloat16)
    shared_ref[...] = jnp.zeros_like(shared_ref)
    embed_ref[...] = jnp.zeros_like(embed_ref)
    for c in range(2):
        piece = lambda i: w_text[:, 2 * half * i + half * c : 2 * half * i + half * (c + 1)].astype(jnp.float32)
        upper = jnp.concatenate([piece(0), piece(1)], axis=1)
        lower = jnp.concatenate([piece(2), w_text_out[:, half * c : half * (c + 1)].astype(jnp.float32)], axis=1)
        text = jnp.concatenate([upper, lower], axis=0).astype(jnp.bfloat16)
        for y in range(4):
            shared_ref[4 * c + y, :, :1024] = text
            shared_ref[4 * c + y, :rows, 1024:] = w_out[:, 640 * c : 640 * c + 768]
        for t in range(8):
            at = HEAD * (2 * t + c)
            q, k, v = (w_heads[:, width * i + at : width * i + at + HEAD] for i in range(3))
            held[0:rows] = jnp.concatenate([q.astype(jnp.float32), v[:, :40].astype(jnp.float32)], axis=1)
            held[rows : 2 * rows] = jnp.concatenate([k.astype(jnp.float32), v[:, 40:80].astype(jnp.float32)], axis=1)
            rest = jnp.where(lane // 8 == row, dot(v[:, 80:], spread), 0.0)
            held[2 * rows : 2 * rows + 1] = jnp.sum(rest, axis=0, keepdims=True)
            held[2 * rows + 1 :] = listed[...]
            value = held[...].astype(jnp.bfloat16)
            for plane in range(8):
                columns_ref[16 * plane + 8 * c + t] = value
                embed_ref[16 * plane + 8 * c + t, :rows] = w_embed[:, LANES * t : LANES * (t + 1)]


def pack_weights(listed, w_heads, *weights):
    vmem = pl.BlockSpec(memory_space=pltpu.VMEM)
    rows = w_heads.shape[0]
    return pl.pallas_call(
        pack_kernel,
        out_shape=(
            jax.ShapeDtypeStruct((8, 16, 1792), jnp.bfloat16),
            jax.ShapeDtypeStruct((128, 2 * rows + 2, LANES), jnp.bfloat16),
            jax.ShapeDtypeStruct((128, 16, LANES), jnp.bfloat16),
        ),
        in_specs=[vmem] * 6,
        out_specs=(vmem,) * 3,
        scratch_shapes=[pltpu.VMEM((2 * rows + 2, LANES), jnp.float32)],
        compiler_params=pltpu.CompilerParams(vmem_limit_bytes=32 * 2**20),
        cost_estimate=pl.CostEstimate(flops=10**6, bytes_accessed=3 * 10**6, transcendentals=0),
        name="pack_weights",
    )(listed, w_heads, *weights)


def per_device(
    video_tokens,
    text_tokens,
    block_lists,
    positive_text,
    video_gain,
    w_video_qkv,
    w_video_out,
    text_gain,
    w_text_qkv,
    w_text_out,
    w_embed,
    gem_power,
    log_scale,
    logit_bias,
):
    h, c = lax.axis_index("h"), lax.axis_index("c")
    x, y, l = lax.axis_index("x"), lax.axis_index("y"), lax.axis_index("l")
    t = 2 * y + l
    flat = video_tokens[0]

    normed = norm_rows(flat, video_gain)
    up = [(i, (i + 1) % 4) for i in range(4)]
    down = [(i, (i - 1) % 4) for i in range(4)]
    own_m = lax.ppermute(normed, "y", up)
    own_p = lax.ppermute(normed, "y", down)
    par = swap(normed, "l")

    listed = jnp.pad(block_lists[0].astype(jnp.float32), ((0, 0), (0, LANES - 8)))
    shared, columns, embed = pack_weights(listed, w_video_qkv, w_video_out, w_embed, w_text_qkv, w_text_out)
    shared = lax.all_to_all(shared, ("c", "y"), 0, 0)
    shared, columns, own_m, own_p, par = lax.optimization_barrier((shared, columns, own_m, own_p, par))
    own_o = lax.ppermute(own_m, "y", up)
    par_m = swap(own_m, "l")
    par_p = lax.ppermute(par, "y", down)
    w_out = shared[:, :12, 1024:].reshape(2 * PIECE, 768)
    out_l = swap(w_out, "l")
    par_p, par_m = lax.optimization_barrier((par_p, par_m))
    par_o = lax.ppermute(par_p, "y", down)

    text = jnp.transpose(shared[:, :, :1024].reshape(8, 2, 8, 1024), (0, 2, 1, 3)).reshape(64, 2048)
    text = lax.all_gather(text, ("x", "h", "l"), axis=0, tiled=True)

    columns = lax.all_to_all(columns, AXES, 0, 0)
    columns, own_o, par_o, out_l = lax.optimization_barrier((columns, own_o, par_o, out_l))
    w_out = jnp.stack([w_out, out_l])
    out_h = swap(w_out, "h")
    count = w_video_qkv.shape[0]
    lists = columns[:, 2 * count + 1, :8].reshape(16, 8, 8)
    lists = lax.dynamic_index_in_dim(lists, 4 * x + 2 * h + c, 0, keepdims=False).astype(jnp.int32)
    last = jnp.pad(columns[:, 2 * count], ((0, 0), (0, LANES)))
    columns = jnp.concatenate([columns[:, :count], columns[:, count : 2 * count]], axis=2).reshape(-1, 2 * LANES)
    columns = jnp.concatenate([columns, last])
    columns_other = swap(columns, "c")

    arrived = [normed, own_m, own_p, par, par_m, par_p, own_o, par_o]
    turn = lambda dy, other: 2 * ((y + dy) % 4) + (1 - l if other else l)
    turns = [turn(0, 0), turn(3, 0), turn(1, 0), turn(0, 1), turn(3, 1), turn(1, 1), turn(2, 0), turn(2, 1)]
    mine = [c, 2 * h + l, 2 * h + 1 - l, 2 - 2 * h + l, 3 - 2 * h - l]
    places = jnp.stack(turns + mine).astype(jnp.int32)
    qk, vt = video_qkv(places, arrived, columns, columns_other)
    text, qk, vt, out_h = lax.optimization_barrier((text, qk, vt, out_h))
    text_other = swap(text, "c")
    w_out = lax.all_gather(jnp.concatenate([w_out, out_h]), "x", axis=0)
    mixed = video_attend(lists, qk, vt)

    core = c.astype(jnp.int32)[None]
    mixed, tokens = lax.optimization_barrier((mixed, text_tokens))
    mixed = lax.all_to_all(mixed, TM, 0, 0)

    texts, length, twidth = text_tokens.shape
    text_embed = text_layer(
        core, tokens.reshape(texts * length, twidth), text_gain[None], text, text_other
    )
    mixed, text_embed, w_out = lax.optimization_barrier((mixed, text_embed, w_out))
    out_other = swap(w_out, "c")
    sent = jnp.transpose(text_embed.astype(jnp.bfloat16).reshape(texts, 8, LANES), (1, 0, 2))
    sent = jnp.broadcast_to(sent[None], (16,) + sent.shape).reshape(128, texts, LANES)
    sent = lax.all_to_all(jnp.concatenate([sent, embed], axis=1), AXES, 0, 0)
    all_texts = sent[:, :texts].reshape(128 * texts, LANES)
    embed = sent[:, texts : texts + w_embed.shape[0]].reshape(-1, LANES)

    video_out, sums = video_project(places, gem_power, mixed, flat, w_out, out_other)
    sums = sums + swap(sums, "l")
    sums = sums + sum(lax.ppermute(sums, "y", [(i, (i + k) % 4) for i in range(4)]) for k in (1, 2, 3))
    floats = jnp.stack([1.0 / gem_power[0], log_scale[0], logit_bias[0]])
    parts = partial_logits(floats, sums, all_texts, embed, 8 * flat.shape[0])
    parts = lax.all_to_all(parts, TM, 0, 0).reshape(parts.shape)
    video_embed, clip_loss = embed_and_loss(positive_text, floats, parts)
    return (video_out[None], video_embed, text_embed, clip_loss[0])


def solution(mesh):
    fine = Mesh(mesh.devices.reshape(4, 2, 2, 4, 2), AXES)
    everywhere = P(DP + TM, None)
    return jax.shard_map(
        per_device,
        mesh=fine,
        in_specs=(
            P(DP, TM, None),
            P(DP + TM, None, None),
            P(DP, TM, None),
            P(DP),
            P(),
            everywhere,
            everywhere,
            P(),
            everywhere,
            everywhere,
            everywhere,
            P(),
            P(),
            P(),
        ),
        out_specs=(P(DP, TM, None), P(DP, None), everywhere, P(DP)),
        check_vma=False,
    )
```

```python
import functools

import jax
import jax.numpy as jnp
import numpy as np
from jax import lax
from jax.experimental import pallas as pl
from jax.experimental.pallas import tpu as pltpu
from jax.sharding import Mesh
from jax.sharding import PartitionSpec as P

VHEADS = 16
THEADS = 16
HEAD = 88
LANES = 128
PIECE = 48
LOG2E = 1.4426950408889634

AXES = ("x", "h", "c", "y", "l")
DP = ("x", "h", "c")
TM = ("y", "l")
PLANE = ("h", "c", "y", "l")


def norm_rows(values, gain):
    full = values.astype(jnp.float32)
    scale = lax.rsqrt(jnp.mean(full * full, axis=-1, keepdims=True) + 1e-06)
    return (full * scale * gain).astype(jnp.bfloat16)


def swap(value, axis):
    return lax.ppermute(value, axis, [(0, 1), (1, 0)])


def dot(a, b):
    return jnp.dot(a, b, preferred_element_type=jnp.float32)


def dot_t(a, b):
    return lax.dot_general(a, b, (((1,), (1,)), ((), ())), preferred_element_type=jnp.float32)


def value_order():
    order = np.zeros((2 * LANES, 5 * LANES), np.float32)
    for head in range(2):
        for feature in range(HEAD):
            to = feature // 11 % 2 * PIECE + feature // 22 * 12 + feature % 11
            if feature < 80:
                source = LANES * (2 * head + feature // 40) + HEAD + feature % 40
            else:
                source = 4 * LANES + 8 * head + feature - 80
            order[LANES * head + to, source] = 1.0
    return jnp.asarray(order, jnp.bfloat16)


def video_qkv_kernel(places, order_hbm, *refs):
    blocks, own, other, qk_ref, vt_ref, x, w, last, order, sems = refs[:8], *refs[8:]
    wide = 2 * LANES
    depth = w.shape[0]
    core = places[8]
    copies = []
    for side, columns in ((core, own), (1 - core, other)):
        lanes = pl.ds(pl.multiple_of(wide * side, LANES), wide)
        copies.append((columns.at[pl.ds(0, depth)], w.at[:, lanes]))
        copies.append((columns.at[pl.ds(depth, LANES), pl.ds(0, LANES)], last.at[side]))
    copies.append((order_hbm, order))
    for j in range(8):
        copies.append((blocks[j], x.at[j]))
    copies = [pltpu.make_async_copy(a, b, sems.at[n]) for n, (a, b) in enumerate(copies)]
    for copy in copies:
        copy.start()
    group = lax.broadcasted_iota(jnp.int32, (depth, LANES), 0) // 11
    lane = lax.broadcasted_iota(jnp.int32, (depth, LANES), 1)
    row = lax.broadcasted_iota(jnp.int32, (depth, LANES), 0)
    chosen = jnp.where(group == lane, 1.0, 0.0).astype(jnp.bfloat16)
    mine = lane // 8 == row % 11
    source = lax.broadcasted_iota(jnp.int32, (LANES, LANES), 0)
    to = lax.broadcasted_iota(jnp.int32, (LANES, LANES), 1)
    for copy in copies[:4]:
        copy.wait()
    tail = jnp.zeros((depth, LANES), jnp.float32)
    for head in range(2):
        rows_of = jnp.where(mine, dot(chosen, last[head]), 0.0).astype(jnp.bfloat16)
        fold = jnp.where((source % 8 + 8 * head == to) & (source < HEAD), 1.0, 0.0).astype(jnp.bfloat16)
        tail = tail + dot(rows_of, fold)
    tail = tail.astype(jnp.bfloat16)
    for copy in copies[4:]:
        copy.wait()
    rows = x.shape[1]
    tokens = x[...].reshape(8 * rows, depth)
    whole = dot(tokens, w[...]).astype(jnp.bfloat16)
    apart = dot(tokens, tail).astype(jnp.bfloat16)
    is_query = lax.broadcasted_iota(jnp.int32, (rows, LANES), 1) < HEAD
    for j in range(8):
        some = whole[rows * j : rows * (j + 1)]
        at = places[j]
        values = dot_t(order[...], jnp.concatenate([some, apart[rows * j : rows * (j + 1)]], axis=1))
        for head in range(2):
            cols = wide * head
            q = some[:, cols : cols + LANES]
            qk_ref[at, :, cols : cols + LANES] = jnp.where(is_query, q, jnp.zeros_like(q))
            qk_ref[at, :, cols + LANES : cols + wide] = some[:, cols + LANES : cols + wide]
            vt_ref[at, head] = values[LANES * head : LANES * (head + 1)].astype(jnp.bfloat16)


def video_qkv(places, blocks, own, other):
    rows, width = blocks[0].shape
    vmem = pl.BlockSpec(memory_space=pltpu.VMEM)
    return pl.pallas_call(
        video_qkv_kernel,
        out_shape=(
            jax.ShapeDtypeStruct((8, rows, 4 * LANES), jnp.bfloat16),
            jax.ShapeDtypeStruct((8, 2, LANES, rows), jnp.bfloat16),
        ),
        in_specs=[pl.BlockSpec(memory_space=pltpu.SMEM)] + [pl.BlockSpec(memory_space=pl.ANY)] * 11,
        out_specs=(vmem, vmem),
        scratch_shapes=[
            pltpu.VMEM((8, rows, width), jnp.bfloat16),
            pltpu.VMEM((width, 4 * LANES), jnp.bfloat16),
            pltpu.VMEM((2, LANES, LANES), jnp.bfloat16),
            pltpu.VMEM((2 * LANES, 5 * LANES), jnp.bfloat16),
            pltpu.SemaphoreType.DMA((13,)),
        ],
        compiler_params=pltpu.CompilerParams(vmem_limit_bytes=60 * 2**20),
        cost_estimate=pl.CostEstimate(flops=5 * 10**9, bytes_accessed=10**7, transcendentals=0),
        name="video_qkv",
    )(places, value_order(), *blocks, own, other)


def video_attend_kernel(lists, qk_hbm, vt_hbm, out_ref, qk, vt, pairs, scores, tops, totals, accs, sems):
    copies = [pltpu.make_async_copy(qk_hbm, qk, sems.at[0]), pltpu.make_async_copy(vt_hbm, vt, sems.at[1])]
    for copy in copies:
        copy.start()
    rows = qk.shape[1]
    count = jnp.int32(0)
    for i in range(8):
        for k in range(8):
            pairs[0, count] = jnp.int32(i)
            pairs[1, count] = lists[i, k]
            pairs[2, count] = jnp.int32(k == 0)
            count = count + jnp.where(lists[i, k] >= 0, 1, 0)

    for copy in copies:
        copy.wait()
    factor = jnp.float32(LOG2E / HEAD**0.5)

    def score(i, j, head):
        at = 2 * LANES * head
        return dot_t(qk[j, :, at + LANES : at + 2 * LANES], qk[i, :, at : at + LANES])

    for head in range(2):
        scores[0, head] = score(pairs[0, 0], pairs[1, 0], head)

    def one_pair(e, carry):
        slot = lax.rem(e, 2)
        i, j, first = pairs[0, e], pairs[1, e], pairs[2, e] == 1
        later = jnp.minimum(e + 1, count - 1)
        next_i, next_j = pairs[0, later], pairs[1, later]
        for head in range(2):
            ahead = score(next_i, next_j, head)
            s = scores[slot, head]
            top = jnp.where(first, jnp.full((1, rows), -1e30, jnp.float32), tops[head])
            top_new = jnp.maximum(top, jnp.max(s, axis=0, keepdims=True))
            shift = top_new * factor
            weights = jnp.exp2(s * factor - shift)
            old = jnp.exp2(top * factor - shift)
            tops[head] = top_new
            totals[head] = jnp.where(first, 0.0, totals[head]) * old + jnp.sum(weights, axis=0, keepdims=True)
            accs[head] = jnp.where(first, 0.0, accs[head]) * old + dot(vt[j, head], weights.astype(jnp.bfloat16))
            scores[1 - slot, head] = ahead

        @pl.when((e == count - 1) | (next_i != i))
        def _():
            for head in range(2):
                mixed = (accs[head] / totals[head]).astype(jnp.bfloat16)
                for l in range(2):
                    to = 2 * PIECE * l + PIECE * head
                    out_ref[i, to : to + PIECE] = mixed[PIECE * l : PIECE * (l + 1)]

        return carry

    lax.fori_loop(0, count, one_pair, 0)


def video_attend(lists, qk, vt):
    rows = qk.shape[1]
    vmem = pl.BlockSpec(memory_space=pltpu.VMEM)
    return pl.pallas_call(
        video_attend_kernel,
        out_shape=jax.ShapeDtypeStruct((8, 4 * PIECE, rows), jnp.bfloat16),
        in_specs=[pl.BlockSpec(memory_space=pltpu.SMEM)] + [pl.BlockSpec(memory_space=pl.ANY)] * 2,
        out_specs=vmem,
        scratch_shapes=[
            pltpu.VMEM(qk.shape, jnp.bfloat16),
            pltpu.VMEM(vt.shape, jnp.bfloat16),
            pltpu.SMEM((3, 72), jnp.int32),
            pltpu.VMEM((2, 2, rows, rows), jnp.float32),
            pltpu.VMEM((2, 1, rows), jnp.float32),
            pltpu.VMEM((2, 1, rows), jnp.float32),
            pltpu.VMEM((2, LANES, rows), jnp.float32),
            pltpu.SemaphoreType.DMA((2,)),
        ],
        compiler_params=pltpu.CompilerParams(vmem_limit_bytes=60 * 2**20),
        cost_estimate=pl.CostEstimate(flops=4 * 10**9, bytes_accessed=4 * 10**6, transcendentals=5 * 10**6),
        name="video_attend",
    )(lists, qk, vt)


def video_out_kernel(places, power, mixed_hbm, tokens_hbm, own, other, out_ref, sums_ref, w, mixed, tokens, sems):
    c = places[8]
    copies = [(mixed_hbm, mixed), (tokens_hbm, tokens)]
    for n in range(4):
        copies.append((own.at[:, n], w.at[c, :, places[9 + n]]))
        copies.append((other.at[:, n], w.at[1 - c, :, places[9 + n]]))
    copies = [pltpu.make_async_copy(a, b, sems.at[n]) for n, (a, b) in enumerate(copies)]
    for copy in copies:
        copy.start()
    for copy in copies:
        copy.wait()
    p = power[0]
    for half, (low, high, skip) in enumerate(((0, 768, 0), (768, 1408, 128))):
        acc = tokens[:, low:high].astype(jnp.float32)
        total = lax.dot_general(
            mixed[...].reshape(32 * PIECE, mixed.shape[2]),
            w[half].reshape(32 * PIECE, 768)[:, skip:],
            (((0,), (0,)), ((), ())),
            preferred_element_type=jnp.float32,
        )
        out = (acc + total).astype(jnp.bfloat16)
        out_ref[:, low:high] = out
        grown = jnp.exp2(jnp.log2(jnp.maximum(out.astype(jnp.float32), 1e-06)) * p)
        sums_ref[:, low:high] = jnp.broadcast_to(jnp.sum(grown, axis=0, keepdims=True), (8, high - low))


def video_project(places, power, mixed, tokens, own, other):
    rows, width = tokens.shape
    vmem = pl.BlockSpec(memory_space=pltpu.VMEM)
    smem = pl.BlockSpec(memory_space=pltpu.SMEM)
    hbm = pl.BlockSpec(memory_space=pl.ANY)
    return pl.pallas_call(
        video_out_kernel,
        out_shape=(
            jax.ShapeDtypeStruct((rows, width), jnp.bfloat16),
            jax.ShapeDtypeStruct((8, width), jnp.float32),
        ),
        in_specs=[smem, smem, hbm, hbm, hbm, hbm],
        out_specs=(vmem, vmem),
        scratch_shapes=[
            pltpu.VMEM((2, 4, 4, 2 * PIECE, 768), jnp.bfloat16),
            pltpu.VMEM(mixed.shape, jnp.bfloat16),
            pltpu.VMEM(tokens.shape, jnp.bfloat16),
            pltpu.SemaphoreType.DMA((10,)),
        ],
        compiler_params=pltpu.CompilerParams(vmem_limit_bytes=60 * 2**20),
        cost_estimate=pl.CostEstimate(flops=10**9, bytes_accessed=10**7, transcendentals=10**6),
        name="video_out",
    )(places, power, mixed, tokens, own, other)


def in_weight_order(rows):
    source = lax.broadcasted_iota(jnp.int32, (LANES, LANES), 0)
    to = lax.broadcasted_iota(jnp.int32, (LANES, LANES), 1)
    wanted = (source // 8) % 2 * 64 + source // 16 * 8 + source % 8
    order = jnp.where(to == wanted, 1.0, 0.0).astype(jnp.bfloat16)
    parts = [dot(rows[:, at : at + LANES], order).astype(jnp.bfloat16) for at in range(0, rows.shape[1], LANES)]
    return jnp.concatenate(parts, axis=1)


def text_kernel(core, tokens_ref, gain_ref, own, other, embed_ref, w, mixed, sems):
    c = core[0]
    sides = (c, 1 - c)
    copies = [pltpu.make_async_copy(part, w.at[side], sems.at[n]) for n, (part, side) in enumerate(zip((own, other), sides))]
    for copy in copies:
        copy.start()
    rows, width = tokens_ref.shape
    half = width // 2
    length = 64
    tile = 256
    tokens = tokens_ref[...].astype(jnp.float32)
    scale = lax.rsqrt(jnp.mean(tokens * tokens, axis=-1, keepdims=True) + 1e-06)
    normed = in_weight_order((tokens * scale * gain_ref[...]).astype(jnp.bfloat16))
    same = (lax.broadcasted_iota(jnp.int32, (2 * tile, tile), 0) % tile // length) == (
        lax.broadcasted_iota(jnp.int32, (2 * tile, tile), 1) // length
    )
    low = lax.broadcasted_iota(jnp.int32, (tile, LANES), 1) < length
    factor = jnp.float32(LOG2E / 8.0)
    for copy, side in zip(copies, sides):
        copy.wait()
        qkv = dot(normed, w[side, :, : 3 * half]).astype(jnp.bfloat16)
        for pair in range(half // LANES):
            at = pair * LANES
            to = pl.ds(pl.multiple_of(side * half + at, LANES), LANES)
            for sub in range(0, rows, tile):
                q = qkv[sub : sub + tile, at : at + LANES]
                key = qkv[sub : sub + tile, half + at : half + at + LANES]
                value = qkv[sub : sub + tile, 2 * half + at : 2 * half + at + LANES]
                none = jnp.zeros_like(q)
                s = dot_t(jnp.concatenate([jnp.where(low, q, none), jnp.where(low, none, q)], axis=0), key)
                s = jnp.where(same, s, jnp.float32(-1e30))
                top = jnp.max(s, axis=1, keepdims=True)
                weights = jnp.exp2((s - top) * factor)
                total = jnp.sum(weights, axis=1, keepdims=True)
                o = dot(weights.astype(jnp.bfloat16), value) / total
                mixed[sub : sub + tile, to] = jnp.where(low, o[:tile], o[tile:]).astype(jnp.bfloat16)
    whole = in_weight_order(mixed[...])
    means = []
    square = jnp.zeros((rows // length, 1), jnp.float32)
    for side in range(2):
        cols = slice(side * half, (side + 1) * half)
        projected = dot(whole, w[side, :, 3 * half :])
        out = (tokens_ref[:, cols].astype(jnp.float32) + projected).astype(jnp.bfloat16).astype(jnp.float32)
        mean = jnp.sum(out.reshape(rows // length, length, half), axis=1) * (1.0 / length)
        square = square + jnp.sum(mean * mean, axis=1, keepdims=True)
        means.append(mean)
    inverse = lax.rsqrt(square + 1e-06)
    for side in range(2):
        embed_ref[:, side * half : (side + 1) * half] = means[side] * inverse


def text_layer(core, tokens, gain, own, other):
    rows, width = tokens.shape
    vmem = pl.BlockSpec(memory_space=pltpu.VMEM)
    hbm = pl.BlockSpec(memory_space=pl.ANY)
    return pl.pallas_call(
        text_kernel,
        out_shape=jax.ShapeDtypeStruct((rows // 64, width), jnp.float32),
        in_specs=[pl.BlockSpec(memory_space=pltpu.SMEM), vmem, vmem, hbm, hbm],
        out_specs=vmem,
        scratch_shapes=[
            pltpu.VMEM((2,) + own.shape, jnp.bfloat16),
            pltpu.VMEM((rows, width), jnp.bfloat16),
            pltpu.SemaphoreType.DMA((2,)),
        ],
        compiler_params=pltpu.CompilerParams(vmem_limit_bytes=50 * 2**20),
        cost_estimate=pl.CostEstimate(flops=17 * 10**9, bytes_accessed=10**7, transcendentals=4 * 10**6),
        name="text_layer",
    )(core, tokens, gain, own, other)


def logits_kernel(floats, sums, texts, columns, out_ref, *, tokens):
    total = sums[0:1]
    pooled = jnp.exp(jnp.log(total * (1.0 / tokens)) * floats[0]).astype(jnp.bfloat16)
    proj = dot(jnp.broadcast_to(pooled, (16, pooled.shape[1])), columns[...])[:8]
    count = texts.shape[0]
    parts = []
    rest = proj
    for _ in range(3):
        parts.append(rest.astype(jnp.bfloat16).astype(jnp.float32))
        rest = rest - parts[-1]
    raw = dot_t(jnp.concatenate(parts + [jnp.zeros_like(proj)], axis=0).astype(jnp.bfloat16), texts[...])
    out_ref[:, 0, :count] = raw[:8] + (raw[8:16] + raw[16:24])
    out_ref[:, 0, count:] = proj


def partial_logits(floats, sums, texts, columns, tokens):
    smem = pl.BlockSpec(memory_space=pltpu.SMEM)
    vmem = pl.BlockSpec(memory_space=pltpu.VMEM)
    return pl.pallas_call(
        functools.partial(logits_kernel, tokens=tokens),
        out_shape=jax.ShapeDtypeStruct((8, 1, texts.shape[0] + LANES), jnp.float32),
        in_specs=[smem, vmem, vmem, vmem],
        out_specs=vmem,
        compiler_params=pltpu.CompilerParams(vmem_limit_bytes=32 * 2**20),
        cost_estimate=pl.CostEstimate(flops=10**7, bytes_accessed=10**6, transcendentals=10**4),
        name="partial_logits",
    )(floats, sums, texts, columns)


def loss_kernel(positive, floats, parts, embed_ref, loss_ref):
    count = parts.shape[2] - LANES
    proj = parts[:, 0, count:]
    inverse = lax.rsqrt(jnp.sum(proj * proj, keepdims=True) + 1e-06)
    for t in range(8):
        embed_ref[:, LANES * t : LANES * (t + 1)] = proj[t : t + 1] * inverse
    raw = jnp.sum(parts[:, 0, :count], axis=0, keepdims=True)
    logits = raw * (inverse * jnp.exp(jnp.full((1, 1), floats[1]))) + floats[2]
    ids = lax.broadcasted_iota(jnp.int32, (1, count), 1)
    z = jnp.where(ids == positive[0], -logits, logits)
    terms = jnp.maximum(z, 0.0) + jnp.log1p(jnp.exp(-jnp.abs(z)))
    loss_ref[...] = jnp.sum(terms, axis=1, keepdims=True) * (1.0 / 128.0)


def embed_and_loss(positive, floats, parts):
    smem = pl.BlockSpec(memory_space=pltpu.SMEM)
    vmem = pl.BlockSpec(memory_space=pltpu.VMEM)
    return pl.pallas_call(
        loss_kernel,
        out_shape=(
            jax.ShapeDtypeStruct((1, 8 * LANES), jnp.float32),
            jax.ShapeDtypeStruct((1, 1), jnp.float32),
        ),
        in_specs=[smem, smem, vmem],
        out_specs=(vmem, vmem),
        cost_estimate=pl.CostEstimate(flops=10**6, bytes_accessed=10**5, transcendentals=10**4),
        name="embed_and_loss",
    )(positive, floats, parts)


def pack_kernel(listed, w_heads, w_out, w_embed, w_text, w_text_out, shared_ref, columns_ref, embed_ref, held):
    rows = w_heads.shape[0]
    half = w_text_out.shape[1] // 2
    width = w_heads.shape[1] // 3
    lane = lax.broadcasted_iota(jnp.int32, (rows, LANES), 1)
    row = lax.broadcasted_iota(jnp.int32, (rows, LANES), 0)
    spread = jnp.where(
        lax.broadcasted_iota(jnp.int32, (8, LANES), 1) % 8 == lax.broadcasted_iota(jnp.int32, (8, LANES), 0), 1.0, 0.0
    ).astype(jnp.bfloat16)
    shared_ref[...] = jnp.zeros_like(shared_ref)
    embed_ref[...] = jnp.zeros_like(embed_ref)
    for c in range(2):
        piece = lambda i: w_text[:, 2 * half * i + half * c : 2 * half * i + half * (c + 1)].astype(jnp.float32)
        upper = jnp.concatenate([piece(0), piece(1)], axis=1)
        lower = jnp.concatenate([piece(2), w_text_out[:, half * c : half * (c + 1)].astype(jnp.float32)], axis=1)
        text = jnp.concatenate([upper, lower], axis=0).astype(jnp.bfloat16)
        for y in range(4):
            shared_ref[4 * c + y, :, :1024] = text
            shared_ref[4 * c + y, :rows, 1024:] = w_out[:, 640 * c : 640 * c + 768]
        for t in range(8):
            at = HEAD * (2 * t + c)
            q, k, v = (w_heads[:, width * i + at : width * i + at + HEAD] for i in range(3))
            held[0:rows] = jnp.concatenate([q.astype(jnp.float32), v[:, :40].astype(jnp.float32)], axis=1)
            held[rows : 2 * rows] = jnp.concatenate([k.astype(jnp.float32), v[:, 40:80].astype(jnp.float32)], axis=1)
            rest = jnp.where(lane // 8 == row, dot(v[:, 80:], spread), 0.0)
            held[2 * rows : 2 * rows + 1] = jnp.sum(rest, axis=0, keepdims=True)
            held[2 * rows + 1 :] = listed[...]
            value = held[...].astype(jnp.bfloat16)
            for plane in range(8):
                columns_ref[16 * plane + 8 * c + t] = value
                embed_ref[16 * plane + 8 * c + t, :rows] = w_embed[:, LANES * t : LANES * (t + 1)]


def pack_weights(listed, w_heads, *weights):
    vmem = pl.BlockSpec(memory_space=pltpu.VMEM)
    rows = w_heads.shape[0]
    return pl.pallas_call(
        pack_kernel,
        out_shape=(
            jax.ShapeDtypeStruct((8, 16, 1792), jnp.bfloat16),
            jax.ShapeDtypeStruct((128, 2 * rows + 2, LANES), jnp.bfloat16),
            jax.ShapeDtypeStruct((128, 16, LANES), jnp.bfloat16),
        ),
        in_specs=[vmem] * 6,
        out_specs=(vmem,) * 3,
        scratch_shapes=[pltpu.VMEM((2 * rows + 2, LANES), jnp.float32)],
        compiler_params=pltpu.CompilerParams(vmem_limit_bytes=32 * 2**20),
        cost_estimate=pl.CostEstimate(flops=10**6, bytes_accessed=3 * 10**6, transcendentals=0),
        name="pack_weights",
    )(listed, w_heads, *weights)


def per_device(
    video_tokens,
    text_tokens,
    block_lists,
    positive_text,
    video_gain,
    w_video_qkv,
    w_video_out,
    text_gain,
    w_text_qkv,
    w_text_out,
    w_embed,
    gem_power,
    log_scale,
    logit_bias,
):
    h, c = lax.axis_index("h"), lax.axis_index("c")
    x, y, l = lax.axis_index("x"), lax.axis_index("y"), lax.axis_index("l")
    t = 2 * y + l
    flat = video_tokens[0]

    normed = norm_rows(flat, video_gain)
    up = [(i, (i + 1) % 4) for i in range(4)]
    down = [(i, (i - 1) % 4) for i in range(4)]
    own_m = lax.ppermute(normed, "y", up)
    own_p = lax.ppermute(normed, "y", down)
    par = swap(normed, "l")

    listed = jnp.pad(block_lists[0].astype(jnp.float32), ((0, 0), (0, LANES - 8)))
    shared, columns, embed = pack_weights(listed, w_video_qkv, w_video_out, w_embed, w_text_qkv, w_text_out)
    shared = lax.all_to_all(shared, ("c", "y"), 0, 0)
    shared, columns, own_m, own_p, par = lax.optimization_barrier((shared, columns, own_m, own_p, par))
    own_o = lax.ppermute(own_m, "y", up)
    par_m = swap(own_m, "l")
    par_p = lax.ppermute(par, "y", down)
    w_out = shared[:, :12, 1024:].reshape(2 * PIECE, 768)
    par_m, w_out = lax.optimization_barrier((par_m, w_out))
    out_l = swap(w_out, "l")
    par_o = lax.ppermute(par_p, "y", down)

    text = jnp.transpose(shared[:, :, :1024].reshape(8, 2, 8, 1024), (0, 2, 1, 3)).reshape(64, 2048)
    text = lax.all_gather(text, ("x", "h", "l"), axis=0, tiled=True)

    columns = lax.all_to_all(columns, AXES, 0, 0)
    columns, own_o, par_o, out_l = lax.optimization_barrier((columns, own_o, par_o, out_l))
    w_out = jnp.stack([w_out, out_l])
    out_h = swap(w_out, "h")
    count = w_video_qkv.shape[0]
    lists = columns[:, 2 * count + 1, :8].reshape(16, 8, 8)
    lists = lax.dynamic_index_in_dim(lists, 4 * x + 2 * h + c, 0, keepdims=False).astype(jnp.int32)
    last = jnp.pad(columns[:, 2 * count], ((0, 0), (0, LANES)))
    columns = jnp.concatenate([columns[:, :count], columns[:, count : 2 * count]], axis=2).reshape(-1, 2 * LANES)
    columns = jnp.concatenate([columns, last])
    columns_other = swap(columns, "c")

    arrived = [normed, own_m, own_p, par, par_m, par_p, own_o, par_o]
    turn = lambda dy, other: 2 * ((y + dy) % 4) + (1 - l if other else l)
    turns = [turn(0, 0), turn(3, 0), turn(1, 0), turn(0, 1), turn(3, 1), turn(1, 1), turn(2, 0), turn(2, 1)]
    mine = [c, 2 * h + l, 2 * h + 1 - l, 2 - 2 * h + l, 3 - 2 * h - l]
    places = jnp.stack(turns + mine).astype(jnp.int32)
    qk, vt = video_qkv(places, arrived, columns, columns_other)
    text, qk, vt, out_h, lists = lax.optimization_barrier((text, qk, vt, out_h, lists))
    text_other = swap(text, "c")
    w_out = lax.all_gather(jnp.concatenate([w_out, out_h]), "x", axis=0)
    mixed = video_attend(lists, qk, vt)

    core = c.astype(jnp.int32)[None]
    mixed, tokens = lax.optimization_barrier((mixed, text_tokens))
    mixed = lax.all_to_all(mixed, TM, 0, 0)

    texts, length, twidth = text_tokens.shape
    text_embed = text_layer(
        core, tokens.reshape(texts * length, twidth), text_gain[None], text, text_other
    )
    mixed, text_embed, w_out = lax.optimization_barrier((mixed, text_embed, w_out))
    out_other = swap(w_out, "c")
    sent = jnp.transpose(text_embed.astype(jnp.bfloat16).reshape(texts, 8, LANES), (1, 0, 2))
    sent = jnp.broadcast_to(sent[None], (16,) + sent.shape).reshape(128, texts, LANES)
    sent = lax.all_to_all(jnp.concatenate([sent, embed], axis=1), AXES, 0, 0)
    all_texts = sent[:, :texts].reshape(128 * texts, LANES)
    embed = sent[:, texts : texts + w_embed.shape[0]].reshape(-1, LANES)

    video_out, sums = video_project(places, gem_power, mixed, flat, w_out, out_other)
    sums = sums + swap(sums, "l")
    sums = sums + sum(lax.ppermute(sums, "y", [(i, (i + k) % 4) for i in range(4)]) for k in (1, 2, 3))
    floats = jnp.stack([1.0 / gem_power[0], log_scale[0], logit_bias[0]])
    parts = partial_logits(floats, sums, all_texts, embed, 8 * flat.shape[0])
    parts = lax.all_to_all(parts, TM, 0, 0).reshape(parts.shape)
    video_embed, clip_loss = embed_and_loss(positive_text, floats, parts)
    return (video_out[None], video_embed, text_embed, clip_loss[0])


def solution(mesh):
    fine = Mesh(mesh.devices.reshape(4, 2, 2, 4, 2), AXES)
    everywhere = P(DP + TM, None)
    return jax.shard_map(
        per_device,
        mesh=fine,
        in_specs=(
            P(DP, TM, None),
            P(DP + TM, None, None),
            P(DP, TM, None),
            P(DP),
            P(),
            everywhere,
            everywhere,
            P(),
            everywhere,
            everywhere,
            everywhere,
            P(),
            P(),
            P(),
        ),
        out_specs=(P(DP, TM, None), P(DP, None), everywhere, P(DP)),
        check_vma=False,
    )
```
